128 devices in a mesh: tm: 8 (over z, core), map: 16 (over x, y).
Axes of the slice: x: 4, y: 4, z: 4, core: 2. Of those that a mesh axis runs over, the one named last changes fastest.
Arguments:
- points: float32 [3, 524288, 128], P(None, ('tm', 'map')), may hold values from -6 to 6
- poses: float32 [6, 4096], P(None, ('tm', 'map')), may hold values from -1.5 to 1.5
- normal_angles: float32 [2, 32768], P(None, ('tm', 'map')), may hold values from -3.140625 to 3.140625
- voxel_ids: int32 [524288], P(('tm', 'map')), may hold values from -1 to 32767, as said below
- scan_ids: int32 [524288], P(('tm', 'map')), may hold values from 0 to 511
Outputs:
- hessian: float32 [36, 4096], P(None, ('tm', 'map'))
- gradient: float32 [6, 4096], P(None, ('tm', 'map'))
- plane_cost: float32 [32768], P(('tm', 'map'))
The draws below stay inside these ranges and needn't reach their ends.
Inputs may be any that keep to these rules, and one draw needn't show every extreme that they name: `voxel_ids`: -1 marks an empty slot. Otherwise the block at position s among the 4096 blocks of its device has its voxel among those of owner o = s // 32, that is, in [o * 256, (o + 1) * 256), where owners are devices in tm+map order. In every draw some owner gets a live block in every slot from every device.
All inputs are finite; a program needn't handle non-finite values.
Results may differ from the reference program's by a relative error of at most 0.0003.
Values sent between devices are 32-bit elements; how exact they have to be, the bound alone decides.
No kernel may reach another device: no remote copies, remote signals or barrier semaphores. Data moves between devices by JAX's collectives and lax.ppermute only.
A program may use at most 128 MiB of HBM per device.

```python
import jax
import jax.numpy as jnp
from jax import lax

PTS = 128
CAP = 32
VOX_DEV = 256
BLK_DEV = 4096
BLOCKS = 524288
VOXELS = 32768
SCAN_ROW = 512
SCANS = 4096
N_MAP = 16
DEVICES = 128


def draw_voxel_ids(key, part):
    keys = jax.random.split(jax.random.fold_in(key, 71), 5)
    slot = jnp.arange(BLOCKS, dtype=jnp.int32)
    owner_of = slot % BLK_DEV // CAP
    hottest = jax.random.randint(keys[0], (), 0, DEVICES)
    level = jax.random.randint(keys[1], (DEVICES,), 3, 10)
    level = jnp.where(jnp.arange(DEVICES, dtype=jnp.int32) == hottest, 10, level)
    coin = jax.random.randint(keys[2], (BLOCKS,), 0, 10)
    first = jax.random.randint(keys[3], (BLOCKS,), 0, VOX_DEV)
    second = jax.random.randint(keys[4], (BLOCKS,), 0, VOX_DEV)
    picked = jnp.minimum(first, second)
    return jnp.where(coin < level[owner_of], owner_of * VOX_DEV + picked, -1).astype(jnp.int32)


def with_ends(result, stream_key, smallest, high):
    longest = result.shape.index(max(result.shape))
    spots = []
    for shift in (0, 1):
        where = [jax.random.randint(jax.random.fold_in(stream_key, axis), (), 0, length) for axis, length in enumerate(result.shape)]
        where[longest] = (where[longest] + shift) % result.shape[longest]
        spots.append(tuple(where))
    return result.at[spots[0]].set(smallest).at[spots[1]].set(high)


def block_scale(rng, extent, shards, smallest, top_value):
    def one(axis_at, parts):
        heights = jax.random.uniform(jax.random.fold_in(jax.random.fold_in(rng, 6), axis_at), (parts,), jnp.float32, smallest / len(shards), top_value / len(shards))
        return jnp.repeat(jnp.exp(heights), extent[axis_at] // parts).reshape((-1,) + (1,) * (len(extent) - axis_at - 1))

    factor_of = one(*shards[0])
    for cut in shards[1:]:
        factor_of = factor_of * one(*cut)
    return factor_of


def normal_values(stream_key, extent, spread, reach, shards=(), held_as=jnp.bfloat16):
    drawn = jax.random.normal(stream_key, extent, jnp.float32) * spread
    if len(shards) > 0:
        drawn = block_scale(stream_key, extent, shards, -0.22, 0.18) * drawn
    return jnp.clip(drawn, min=-reach, max=reach).astype(held_as)


def setup_inputs(seed: int = 0) -> dict:
    splits = jax.random.split(jax.random.key(seed), 6)
    return {
        "points": normal_values(splits[0], (3, BLOCKS, PTS), 1.0, 6.0, ((1, 128),), jnp.float32),
        "poses": jnp.clip(jax.random.uniform(splits[1], (6, SCANS), jnp.float32, -1.5, 1.5) * block_scale(splits[1], (6, SCANS), ((1, 128),), -0.4, 0.0), -1.5, 1.5),
        "normal_angles": jnp.clip(jax.random.uniform(splits[2], (2, VOXELS), jnp.float32, -3.140625, 3.140625), -3.140625, 3.140625),
        "voxel_ids": draw_voxel_ids(jax.random.fold_in(splits[5], 71), 0),
        "scan_ids": with_ends(jax.random.randint(splits[4], (BLOCKS,), 0, SCAN_ROW), jax.random.fold_in(splits[4], 1), 0, SCAN_ROW - 1).astype(jnp.int32),
    }


def rigid(angles):
    cos_x, sin_x = jnp.cos(angles[0]), jnp.sin(angles[0])
    cos_y, sin_y = jnp.cos(angles[1]), jnp.sin(angles[1])
    cos_z, sin_z = jnp.cos(angles[2]), jnp.sin(angles[2])
    return jnp.stack([
        cos_z * cos_y, cos_z * sin_y * sin_x - sin_z * cos_x, cos_z * sin_y * cos_x + sin_z * sin_x,
        sin_z * cos_y, sin_z * sin_y * sin_x + cos_z * cos_x, sin_z * sin_y * cos_x - cos_z * sin_x,
        -sin_y, cos_y * sin_x, cos_y * cos_x,
        angles[3], angles[4], angles[5]])


def transform(points, per_block):
    rows_out = []
    for axis_out in range(3):
        acc = per_block[9 + axis_out][:, None]
        for axis_in in range(3):
            acc = acc + per_block[3 * axis_out + axis_in][:, None] * points[axis_in]
        rows_out.append(acc)
    return jnp.stack(rows_out)


def moments_of(world_pts):
    first = jnp.sum(world_pts, axis=2)
    pairs = [(0, 0), (1, 1), (2, 2), (0, 1), (0, 2), (1, 2)]
    second = jnp.stack([jnp.sum(world_pts[i] * world_pts[j], axis=1) for i, j in pairs])
    return jnp.concatenate([first, second], axis=0)


def unit_normal(normal_angles):
    theta, phi = normal_angles[0], normal_angles[1]
    return jnp.stack([jnp.sin(theta) * jnp.cos(phi), jnp.sin(theta) * jnp.sin(phi), jnp.cos(theta)])


def block_terms(world_pts, normal, offset):
    cross = jnp.stack([
        world_pts[1] * normal[2][:, None] - world_pts[2] * normal[1][:, None],
        world_pts[2] * normal[0][:, None] - world_pts[0] * normal[2][:, None],
        world_pts[0] * normal[1][:, None] - world_pts[1] * normal[0][:, None]])
    normal_b = jnp.broadcast_to(normal[:, :, None], world_pts.shape)
    jacobian = jnp.concatenate([cross, normal_b], axis=0)
    resid = jnp.sum(world_pts * normal[:, :, None], axis=0) - offset[:, None]
    outer = jnp.einsum('ibp,jbp->ijb', jacobian, jacobian, precision=lax.Precision.HIGHEST)
    grad_b = jnp.einsum('ibp,bp->ib', jacobian, resid, precision=lax.Precision.HIGHEST)
    return jnp.concatenate([outer.reshape(36, -1), grad_b], axis=0)


def reference(points, poses, normal_angles, voxel_ids, scan_ids):
    pose_table = rigid(poses)
    block_index = jnp.arange(BLOCKS, dtype=jnp.int32)
    global_scan = (block_index // BLK_DEV // N_MAP) * SCAN_ROW + scan_ids
    is_live = voxel_ids >= 0

    def span_world(index):
        start = (index * BLK_DEV).astype(jnp.int32)
        pts = lax.dynamic_slice_in_dim(points, start, BLK_DEV, 1)
        scans = lax.dynamic_slice_in_dim(global_scan, start, BLK_DEV, 0)
        return transform(pts, pose_table[:, scans])

    def span_moments(index):
        start = (index * BLK_DEV).astype(jnp.int32)
        live_c = lax.dynamic_slice_in_dim(is_live, start, BLK_DEV, 0)
        return jnp.where(live_c[None, :], moments_of(span_world(index)), 0.0)

    moments = lax.map(span_moments, jnp.arange(DEVICES, dtype=jnp.int32))
    moments = jnp.transpose(moments, (0, 2, 1)).reshape(BLOCKS, 9)
    segment = jnp.where(is_live, voxel_ids, VOXELS)
    voxel_sums = jax.ops.segment_sum(moments, segment, num_segments=VOXELS + 1)[:VOXELS].T
    counts = jax.ops.segment_sum(is_live.astype(jnp.float32), segment, num_segments=VOXELS + 1)[:VOXELS] * PTS
    floor_count = jnp.maximum(counts, 1.0)
    normal = unit_normal(normal_angles)
    offset = jnp.sum(normal * voxel_sums[:3], axis=0) / floor_count
    quadric = (normal[0] ** 2 * voxel_sums[3] + normal[1] ** 2 * voxel_sums[4] + normal[2] ** 2 * voxel_sums[5]
               + 2.0 * (normal[0] * normal[1] * voxel_sums[6] + normal[0] * normal[2] * voxel_sums[7]
                        + normal[1] * normal[2] * voxel_sums[8]))
    plane_cost = quadric / floor_count - offset ** 2
    safe_ids = jnp.where(is_live, voxel_ids, 0)
    block_normal = jnp.where(is_live[None, :], normal[:, safe_ids], 0.0)
    block_offset = jnp.where(is_live, offset[safe_ids], 0.0)

    def span_terms(index):
        start = (index * BLK_DEV).astype(jnp.int32)
        norm_c = lax.dynamic_slice_in_dim(block_normal, start, BLK_DEV, 1)
        off_c = lax.dynamic_slice_in_dim(block_offset, start, BLK_DEV, 0)
        return block_terms(span_world(index), norm_c, off_c)

    terms = lax.map(span_terms, jnp.arange(DEVICES, dtype=jnp.int32))
    terms = jnp.transpose(terms, (0, 2, 1)).reshape(BLOCKS, 42)
    per_scan = jax.ops.segment_sum(terms, global_scan, num_segments=SCANS).T
    per_scan = per_scan * (SCANS / (BLOCKS * PTS))
    return per_scan[:36], per_scan[36:], plane_cost
```

```python
import functools

import jax
import jax.numpy as jnp
from jax import lax
from jax.experimental import pallas as pl
from jax.experimental.pallas import tpu as pltpu
from jax.sharding import PartitionSpec as P

LANES = 128
GROUPS = 4
SLOTS = 32
PTS = 128
SENT_ROWS = 5
ROWS = 32
TM = 8
SCAN_ROW = 512
VOX = 256
BF16 = jnp.bfloat16
F32 = jnp.float32


def swap_groups(rows):
    lane = lax.broadcasted_iota(jnp.int32, rows[0].shape, 1) // SLOTS
    out = []
    for g in range(GROUPS):
        acc = None
        for h in range(GROUPS):
            shift = (h - g) * SLOTS % LANES
            part = rows[h] if shift == 0 else pltpu.roll(rows[h], shift, 1)
            acc = part if acc is None else jnp.where(lane == h, part, acc)
        out.append(acc)
    return out


def split3(x):
    hi = x.astype(BF16)
    rest = x - hi.astype(F32)
    mid = rest.astype(BF16)
    lo = (rest - mid.astype(F32)).astype(BF16)
    return jnp.concatenate([hi, mid, lo], axis=0)


def fold3(x):
    n = x.shape[0] // 3
    return x[:n] + x[n : 2 * n] + x[2 * n :]


def moments_kernel(points_ref, vox_ref, scan_ref, poses_ref, sent_ref, acc_ref):
    step = pl.program_id(0)
    chunks = points_ref.shape[1] // LANES
    for cc in range(chunks):
        span = pl.ds(cc * LANES, LANES)
        x = points_ref[0, span, :].T
        y = points_ref[1, span, :].T
        z = points_ref[2, span, :].T
        quantities = [x, y, z, x * x, y * y, z * z, x * y, x * z, y * z]
        for f, q in enumerate(quantities):
            acc_ref[f, pl.ds(step * chunks + cc, 1), :] = jnp.sum(q, axis=0, keepdims=True)

    @pl.when(step == pl.num_programs(0) - 1)
    def _():
        lane = lax.broadcasted_iota(jnp.int32, (ROWS, LANES), 1)
        row = lax.broadcasted_iota(jnp.int32, (ROWS, LANES), 0)
        vox = vox_ref[...]
        owner = row * GROUPS + lane // SLOTS
        vox = jnp.where(vox >= 0, vox - owner * VOX, -1).astype(F32)
        scan = scan_ref[...].astype(F32)
        p = poses_ref[...]
        p = jnp.concatenate([p, p, p, p], axis=1)
        cos, sin = jnp.cos(p[:3]), jnp.sin(p[:3])
        one = [cos[0:1], sin[0:1], cos[1:2], sin[1:2], cos[2:3], sin[2:3], p[3:4], p[4:5], p[5:6]]
        group = lax.broadcasted_iota(jnp.int32, (1, LANES), 1) // SLOTS
        f = [acc_ref[i] for i in range(9)]
        whole = lambda r: jnp.broadcast_to(r, (ROWS, LANES))
        k0 = swap_groups(f[0:4])
        k1 = swap_groups(f[4:8])
        k2 = swap_groups([f[8], vox, scan, whole(one[0])])

        def four(rs):
            r = jnp.where(group == 0, rs[0], jnp.where(group == 1, rs[1], jnp.where(group == 2, rs[2], rs[3])))
            return whole(r)

        k3 = four(one[1:5])
        k4 = four(one[5:9])
        for g in range(GROUPS):
            for k, v in enumerate([k0[g], k1[g], k2[g], k3, k4]):
                sent_ref[pl.ds(g * SENT_ROWS + k, ROWS, stride=GROUPS * SENT_ROWS), :] = v


def owner_kernel(recv_ref, angles_ref, out_ref, cost_ref, tab_ref, gat_ref, hot_ref, vhot_ref, feat_ref):
    feats = []
    for k in range(SENT_ROWS):
        rows = [recv_ref[pl.ds(h * SENT_ROWS + k, ROWS, stride=GROUPS * SENT_ROWS), :] for h in range(GROUPS)]
        feats += swap_groups(rows)
    p1 = feats[0:3]
    pxx, pyy, pzz, pxy, pxz, pyz = feats[3:9]
    vox = feats[9].astype(jnp.int32)
    scan = feats[10].astype(jnp.int32)
    cx, sx, cy, sy, cz, sz, tx, ty, tz = feats[11:20]
    table = [
        cz * cy,
        cz * sy * sx - sz * cx,
        cz * sy * cx + sz * sx,
        sz * cy,
        sz * sy * sx + cz * cx,
        sz * sy * cx - cz * sx,
        -sy,
        cy * sx,
        cy * cx,
        tx,
        ty,
        tz,
    ]
    zeros = jnp.zeros((ROWS, LANES), F32)
    for f in range(16):
        tab_ref[pl.ds(f, ROWS, stride=16), :] = table[f] if f < 12 else zeros

    def wide(ref, t, n):
        return jnp.concatenate([ref[pl.ds((t * 4 + i) * n, n), :] for i in range(4)], axis=1)

    def put(ref, t, n, val):
        for i in range(4):
            ref[pl.ds((t * 4 + i) * n, n), :] = val[:, i * LANES : (i + 1) * LANES]

    scan_iota = lax.broadcasted_iota(jnp.int32, (SCAN_ROW, LANES), 0)
    vox_iota = lax.broadcasted_iota(jnp.int32, (VOX, LANES), 0)
    for t in range(TM):
        for i in range(4):
            r = 4 * t + i
            hot_ref[t, :, i * LANES : (i + 1) * LANES] = jnp.where(scan_iota == scan[r : r + 1, :], 1.0, 0.0).astype(BF16)
            vhot_ref[:, r * LANES : (r + 1) * LANES] = jnp.where(vox_iota == vox[r : r + 1, :], 1.0, 0.0).astype(BF16)
        got = jnp.dot(split3(wide(tab_ref, t, 16)), hot_ref[t], preferred_element_type=F32)
        put(gat_ref, t, 16, fold3(got))

    rot = [[gat_ref[pl.ds(3 * i + j, ROWS, stride=16), :] for j in range(3)] for i in range(3)]
    tr = [gat_ref[pl.ds(9 + i, ROWS, stride=16), :] for i in range(3)]
    second = [[pxx, pxy, pxz], [pxy, pyy, pyz], [pxz, pyz, pzz]]
    rp = [sum(rot[i][j] * p1[j] for j in range(3)) for i in range(3)]
    half = [[sum(rot[i][k] * second[k][j] for k in range(3)) for j in range(3)] for i in range(3)]
    m1 = [rp[i] + PTS * tr[i] for i in range(3)]
    m2 = {}
    for i, j in [(0, 0), (1, 1), (2, 2), (0, 1), (0, 2), (1, 2)]:
        m2[i, j] = sum(half[i][k] * rot[j][k] for k in range(3)) + rp[i] * tr[j] + tr[i] * m1[j]
        m2[j, i] = m2[i, j]
    world = m1 + [m2[0, 0], m2[1, 1], m2[2, 2], m2[0, 1], m2[0, 2], m2[1, 2], jnp.ones((ROWS, LANES), F32)]
    for f in range(16):
        tab_ref[pl.ds(f, ROWS, stride=16), :] = world[f] if f < 10 else zeros

    nt = (((1,), (1,)), ((), ()))
    sums = jnp.zeros((48, VOX), F32)
    for t in range(TM):
        sums = sums + lax.dot_general(
            split3(wide(tab_ref, t, 16)), vhot_ref[:, t * 512 : (t + 1) * 512], nt, preferred_element_type=F32
        )
    sums = fold3(sums)
    count = jnp.maximum(sums[9:10] * PTS, 1.0)
    angles = angles_ref[...]
    cos, sin = jnp.cos(angles), jnp.sin(angles)
    n = [sin[0:1] * cos[1:2], sin[0:1] * sin[1:2], cos[0:1]]
    offset = (n[0] * sums[0:1] + n[1] * sums[1:2] + n[2] * sums[2:3]) / count
    quadric = (
        n[0] * n[0] * sums[3:4]
        + n[1] * n[1] * sums[4:5]
        + n[2] * n[2] * sums[5:6]
        + 2.0 * (n[0] * n[1] * sums[6:7] + n[0] * n[2] * sums[7:8] + n[1] * n[2] * sums[8:9])
    )
    cost_ref[...] = quadric / count - offset * offset
    plane = split3(jnp.concatenate(n + [offset, jnp.zeros((4, VOX), F32)], axis=0))
    for t in range(TM):
        got = jnp.dot(plane, vhot_ref[:, t * 512 : (t + 1) * 512], preferred_element_type=F32)
        put(gat_ref, t, 8, fold3(got))
    n0, n1, n2, d = [gat_ref[pl.ds(f, ROWS, stride=8), :] for f in range(4)]
    nb = [n0, n1, n2]

    def cross(v):
        return [v[1] * n2 - v[2] * n1, v[2] * n0 - v[0] * n2, v[0] * n1 - v[1] * n0]

    am2 = list(zip(*[cross([m2[0, j], m2[1, j], m2[2, j]]) for j in range(3)]))
    ama = [cross(am2[i]) for i in range(3)]
    am1 = cross(m1)
    terms = {}
    for i in range(3):
        for j in range(i, 3):
            terms[i, j] = ama[i][j]
            terms[3 + i, 3 + j] = PTS * nb[i] * nb[j]
        for j in range(3):
            terms[i, 3 + j] = am1[i] * nb[j]
    resid = sum(nb[i] * m1[i] for i in range(3)) - PTS * d
    grad = [sum(am2[i][j] * nb[j] for j in range(3)) - d * am1[i] for i in range(3)] + [nb[i] * resid for i in range(3)]
    features = [terms[i, j] for i in range(6) for j in range(i, 6)] + grad
    for f in range(32):
        feat_ref[pl.ds(f, ROWS, stride=32), :] = features[f] if f < 27 else zeros
    for t in range(TM):
        ft = wide(feat_ref, t, 32)
        hi = ft.astype(BF16)
        lo = (ft - hi.astype(F32)).astype(BF16)
        got = lax.dot_general(jnp.concatenate([hi, lo], axis=0), hot_ref[t], nt, preferred_element_type=F32)
        got = got[:32] + got[32:]
        for c in range(4):
            part = [got[8 * j : 8 * j + 8, c * LANES : (c + 1) * LANES] for j in range(4)]
            for g, v in enumerate(swap_groups(part)):
                out_ref[t * 16 + 4 * c + g] = v


def scans_kernel(scale, recv_ref, hess_ref, grad_ref):
    total = jnp.sum(recv_ref[...], axis=0) * scale
    part = [total[:, j * SLOTS : (j + 1) * SLOTS] for j in range(4)]
    f = 0
    for i in range(6):
        for j in range(i, 6):
            row = part[f // 8][f % 8 : f % 8 + 1]
            hess_ref[6 * i + j : 6 * i + j + 1, :] = row
            if i != j:
                hess_ref[6 * j + i : 6 * j + i + 1, :] = row
            f += 1
    for i in range(6):
        grad_ref[i : i + 1, :] = part[f // 8][f % 8 : f % 8 + 1]
        f += 1


def local(points, poses, normal_angles, voxel_ids, scan_ids):
    axes = ("tm", "map")
    blocks = points.shape[1]
    devices = lax.axis_size(axes)
    steps = 8
    sent = pl.pallas_call(
        moments_kernel,
        grid=(steps,),
        in_specs=[
            pl.BlockSpec((3, blocks // steps, PTS), lambda i: (0, i, 0)),
            pl.BlockSpec((ROWS, LANES), lambda i: (0, 0)),
            pl.BlockSpec((ROWS, LANES), lambda i: (0, 0)),
            pl.BlockSpec((6, SLOTS), lambda i: (0, 0)),
        ],
        out_specs=pl.BlockSpec((devices * SENT_ROWS, LANES), lambda i: (0, 0)),
        out_shape=jax.ShapeDtypeStruct((devices * SENT_ROWS, LANES), F32),
        scratch_shapes=[pltpu.VMEM((9, ROWS, LANES), F32)],
        compiler_params=pltpu.CompilerParams(vmem_limit_bytes=32 * 1024 * 1024),
    )(points, voxel_ids.reshape(ROWS, LANES), scan_ids.reshape(ROWS, LANES), poses)
    recv = lax.all_to_all(sent.reshape(devices, 1, SENT_ROWS * LANES), axes, 0, 0, tiled=True)
    recv = recv.reshape(devices * SENT_ROWS, LANES)
    shares, cost = pl.pallas_call(
        owner_kernel,
        out_shape=(
            jax.ShapeDtypeStruct((devices, 8, LANES), F32),
            jax.ShapeDtypeStruct((1, VOX), F32),
        ),
        scratch_shapes=[
            pltpu.VMEM((ROWS * 16, LANES), F32),
            pltpu.VMEM((ROWS * 16, LANES), F32),
            pltpu.VMEM((TM, SCAN_ROW, 512), BF16),
            pltpu.VMEM((VOX, 4096), BF16),
            pltpu.VMEM((ROWS * 32, LANES), F32),
        ],
        compiler_params=pltpu.CompilerParams(vmem_limit_bytes=32 * 1024 * 1024),
    )(recv, normal_angles)
    arrived = lax.all_to_all(shares, axes, 0, 0, tiled=True)
    all_scans = poses.shape[1] * devices
    scale = all_scans / (blocks * devices * PTS)
    hess, grad = pl.pallas_call(
        functools.partial(scans_kernel, scale),
        out_shape=(
            jax.ShapeDtypeStruct((36, SLOTS), F32),
            jax.ShapeDtypeStruct((6, SLOTS), F32),
        ),
    )(arrived)
    return hess, grad, cost.reshape(VOX)


def solution(mesh):
    return jax.shard_map(
        local,
        mesh=mesh,
        in_specs=(
            P(None, ("tm", "map"), None),
            P(None, ("tm", "map")),
            P(None, ("tm", "map")),
            P(("tm", "map")),
            P(("tm", "map")),
        ),
        out_specs=(P(None, ("tm", "map")), P(None, ("tm", "map")), P(("tm", "map"))),
        check_vma=False,
    )
```

```python
import functools

import jax
import jax.numpy as jnp
from jax import lax
from jax.experimental import pallas as pl
from jax.experimental.pallas import tpu as pltpu
from jax.sharding import PartitionSpec as P

LANES = 128
GROUPS = 4
SLOTS = 32
PTS = 128
SENT_ROWS = 5
ROWS = 32
TM = 8
SCAN_ROW = 512
VOX = 256
BF16 = jnp.bfloat16
F32 = jnp.float32


def swap_groups(rows):
    lane = lax.broadcasted_iota(jnp.int32, rows[0].shape, 1) // SLOTS
    out = []
    for g in range(GROUPS):
        acc = None
        for h in range(GROUPS):
            shift = (h - g) * SLOTS % LANES
            part = rows[h] if shift == 0 else pltpu.roll(rows[h], shift, 1)
            acc = part if acc is None else jnp.where(lane == h, part, acc)
        out.append(acc)
    return out


def split3(x):
    hi = x.astype(BF16)
    rest = x - hi.astype(F32)
    mid = rest.astype(BF16)
    lo = (rest - mid.astype(F32)).astype(BF16)
    return jnp.concatenate([hi, mid, lo], axis=0)


def fold3(x):
    n = x.shape[0] // 3
    return x[:n] + x[n : 2 * n] + x[2 * n :]


def moments_kernel(points_hbm, vox_hbm, scan_hbm, poses_hbm, sent_ref, acc_ref, points_ref, vox_ref, scan_ref, poses_ref, sems, small_sems):
    chunks = sems.shape[0]
    size = points_ref.shape[1] // chunks

    def fetch(c):
        span = pl.ds(c * size, size)
        return pltpu.make_async_copy(points_hbm.at[:, span, :], points_ref.at[:, span, :], sems.at[c])

    small = [
        pltpu.make_async_copy(vox_hbm, vox_ref, small_sems.at[0]),
        pltpu.make_async_copy(scan_hbm, scan_ref, small_sems.at[1]),
        pltpu.make_async_copy(poses_hbm, poses_ref, small_sems.at[2]),
    ]
    for c in range(chunks):
        fetch(c).start()
    for copy in small:
        copy.start()

    @pl.loop(0, chunks)
    def _(c):
        fetch(c).wait()
        for cc in range(size // LANES):
            span = pl.ds(pl.multiple_of(c * size + cc * LANES, LANES), LANES)
            x = points_ref[0, span, :].T
            y = points_ref[1, span, :].T
            z = points_ref[2, span, :].T
            quantities = [x, y, z, x * x, y * y, z * z, x * y, x * z, y * z]
            for f, q in enumerate(quantities):
                acc_ref[f, pl.ds(c * (size // LANES) + cc, 1), :] = jnp.sum(q, axis=0, keepdims=True)

    for copy in small:
        copy.wait()
    lane = lax.broadcasted_iota(jnp.int32, (ROWS, LANES), 1)
    row = lax.broadcasted_iota(jnp.int32, (ROWS, LANES), 0)
    vox = vox_ref[...]
    owner = row * GROUPS + lane // SLOTS
    vox = jnp.where(vox >= 0, vox - owner * VOX, -1).astype(F32)
    scan = scan_ref[...].astype(F32)
    p = poses_ref[...]
    p = jnp.concatenate([p, p, p, p], axis=1)
    cos, sin = jnp.cos(p[:3]), jnp.sin(p[:3])
    one = [cos[0:1], sin[0:1], cos[1:2], sin[1:2], cos[2:3], sin[2:3], p[3:4], p[4:5], p[5:6]]
    group = lax.broadcasted_iota(jnp.int32, (1, LANES), 1) // SLOTS
    f = [acc_ref[i] for i in range(9)]
    whole = lambda r: jnp.broadcast_to(r, (ROWS, LANES))
    k0 = swap_groups(f[0:4])
    k1 = swap_groups(f[4:8])
    k2 = swap_groups([f[8], vox, scan, whole(one[0])])

    def four(rs):
        r = jnp.where(group == 0, rs[0], jnp.where(group == 1, rs[1], jnp.where(group == 2, rs[2], rs[3])))
        return whole(r)

    k3 = four(one[1:5])
    k4 = four(one[5:9])
    for g in range(GROUPS):
        for k, v in enumerate([k0[g], k1[g], k2[g], k3, k4]):
            sent_ref[pl.ds(g * SENT_ROWS + k, ROWS, stride=GROUPS * SENT_ROWS), :] = v


def owner_kernel(recv_ref, angles_ref, out_ref, cost_ref, tab_ref, gat_ref, hot_ref, vhot_ref, feat_ref):
    feats = []
    for k in range(SENT_ROWS):
        rows = [recv_ref[pl.ds(h * SENT_ROWS + k, ROWS, stride=GROUPS * SENT_ROWS), :] for h in range(GROUPS)]
        feats += swap_groups(rows)
    p1 = feats[0:3]
    pxx, pyy, pzz, pxy, pxz, pyz = feats[3:9]
    vox = feats[9].astype(jnp.int32)
    scan = feats[10].astype(jnp.int32)
    cx, sx, cy, sy, cz, sz, tx, ty, tz = feats[11:20]
    table = [
        cz * cy,
        cz * sy * sx - sz * cx,
        cz * sy * cx + sz * sx,
        sz * cy,
        sz * sy * sx + cz * cx,
        sz * sy * cx - cz * sx,
        -sy,
        cy * sx,
        cy * cx,
        tx,
        ty,
        tz,
    ]
    zeros = jnp.zeros((ROWS, LANES), F32)
    for f in range(16):
        tab_ref[pl.ds(f, ROWS, stride=16), :] = table[f] if f < 12 else zeros

    def wide(ref, t, n):
        return jnp.concatenate([ref[pl.ds((t * 4 + i) * n, n), :] for i in range(4)], axis=1)

    def put(ref, t, n, val):
        for i in range(4):
            ref[pl.ds((t * 4 + i) * n, n), :] = val[:, i * LANES : (i + 1) * LANES]

    scan_iota = lax.broadcasted_iota(jnp.int32, (SCAN_ROW, LANES), 0)
    vox_iota = lax.broadcasted_iota(jnp.int32, (VOX, LANES), 0)
    for t in range(TM):
        for i in range(4):
            r = 4 * t + i
            hot_ref[t, :, i * LANES : (i + 1) * LANES] = jnp.where(scan_iota == scan[r : r + 1, :], 1.0, 0.0).astype(BF16)
            vhot_ref[:, r * LANES : (r + 1) * LANES] = jnp.where(vox_iota == vox[r : r + 1, :], 1.0, 0.0).astype(BF16)
        got = jnp.dot(split3(wide(tab_ref, t, 16)), hot_ref[t], preferred_element_type=F32)
        put(gat_ref, t, 16, fold3(got))

    rot = [[gat_ref[pl.ds(3 * i + j, ROWS, stride=16), :] for j in range(3)] for i in range(3)]
    tr = [gat_ref[pl.ds(9 + i, ROWS, stride=16), :] for i in range(3)]
    second = [[pxx, pxy, pxz], [pxy, pyy, pyz], [pxz, pyz, pzz]]
    rp = [sum(rot[i][j] * p1[j] for j in range(3)) for i in range(3)]
    half = [[sum(rot[i][k] * second[k][j] for k in range(3)) for j in range(3)] for i in range(3)]
    m1 = [rp[i] + PTS * tr[i] for i in range(3)]
    m2 = {}
    for i, j in [(0, 0), (1, 1), (2, 2), (0, 1), (0, 2), (1, 2)]:
        m2[i, j] = sum(half[i][k] * rot[j][k] for k in range(3)) + rp[i] * tr[j] + tr[i] * m1[j]
        m2[j, i] = m2[i, j]
    world = m1 + [m2[0, 0], m2[1, 1], m2[2, 2], m2[0, 1], m2[0, 2], m2[1, 2], jnp.ones((ROWS, LANES), F32)]
    for f in range(16):
        tab_ref[pl.ds(f, ROWS, stride=16), :] = world[f] if f < 10 else zeros

    nt = (((1,), (1,)), ((), ()))
    sums = jnp.zeros((48, VOX), F32)
    for t in range(TM):
        sums = sums + lax.dot_general(
            split3(wide(tab_ref, t, 16)), vhot_ref[:, t * 512 : (t + 1) * 512], nt, preferred_element_type=F32
        )
    sums = fold3(sums)
    count = jnp.maximum(sums[9:10] * PTS, 1.0)
    angles = angles_ref[...]
    cos, sin = jnp.cos(angles), jnp.sin(angles)
    n = [sin[0:1] * cos[1:2], sin[0:1] * sin[1:2], cos[0:1]]
    offset = (n[0] * sums[0:1] + n[1] * sums[1:2] + n[2] * sums[2:3]) / count
    quadric = (
        n[0] * n[0] * sums[3:4]
        + n[1] * n[1] * sums[4:5]
        + n[2] * n[2] * sums[5:6]
        + 2.0 * (n[0] * n[1] * sums[6:7] + n[0] * n[2] * sums[7:8] + n[1] * n[2] * sums[8:9])
    )
    cost_ref[...] = quadric / count - offset * offset
    plane = split3(jnp.concatenate(n + [offset, jnp.zeros((4, VOX), F32)], axis=0))
    for t in range(TM):
        got = jnp.dot(plane, vhot_ref[:, t * 512 : (t + 1) * 512], preferred_element_type=F32)
        put(gat_ref, t, 8, fold3(got))
    n0, n1, n2, d = [gat_ref[pl.ds(f, ROWS, stride=8), :] for f in range(4)]
    nb = [n0, n1, n2]

    def cross(v):
        return [v[1] * n2 - v[2] * n1, v[2] * n0 - v[0] * n2, v[0] * n1 - v[1] * n0]

    am2 = list(zip(*[cross([m2[0, j], m2[1, j], m2[2, j]]) for j in range(3)]))
    ama = [cross(am2[i]) for i in range(3)]
    am1 = cross(m1)
    terms = {}
    for i in range(3):
        for j in range(i, 3):
            terms[i, j] = ama[i][j]
            terms[3 + i, 3 + j] = PTS * nb[i] * nb[j]
        for j in range(3):
            terms[i, 3 + j] = am1[i] * nb[j]
    resid = sum(nb[i] * m1[i] for i in range(3)) - PTS * d
    grad = [sum(am2[i][j] * nb[j] for j in range(3)) - d * am1[i] for i in range(3)] + [nb[i] * resid for i in range(3)]
    features = [terms[i, j] for i in range(6) for j in range(i, 6)] + grad
    for f in range(32):
        feat_ref[pl.ds(f, ROWS, stride=32), :] = features[f] if f < 27 else zeros
    for t in range(TM):
        ft = wide(feat_ref, t, 32)
        hi = ft.astype(BF16)
        lo = (ft - hi.astype(F32)).astype(BF16)
        got = lax.dot_general(jnp.concatenate([hi, lo], axis=0), hot_ref[t], nt, preferred_element_type=F32)
        got = got[:32] + got[32:]
        for c in range(4):
            part = [got[8 * j : 8 * j + 8, c * LANES : (c + 1) * LANES] for j in range(4)]
            for g, v in enumerate(swap_groups(part)):
                out_ref[t * 16 + 4 * c + g] = v


def scans_kernel(scale, recv_ref, hess_ref, grad_ref):
    total = jnp.sum(recv_ref[...], axis=0) * scale
    part = [total[:, j * SLOTS : (j + 1) * SLOTS] for j in range(4)]
    rows = [part[f // 8][f % 8 : f % 8 + 1] for f in range(27)]
    place = {ij: f for f, ij in enumerate([(i, j) for i in range(6) for j in range(i, 6)])}
    hess = [rows[place[min(i, j), max(i, j)]] for i in range(6) for j in range(6)]
    hess_ref[...] = jnp.concatenate(hess, axis=0).T
    grad_ref[...] = jnp.concatenate(rows[21:], axis=0)


def local(points, poses, normal_angles, voxel_ids, scan_ids):
    axes = ("tm", "map")
    blocks = points.shape[1]
    devices = lax.axis_size(axes)
    anywhere = pl.BlockSpec(memory_space=pl.ANY)
    chunks = 8
    sent = pl.pallas_call(
        moments_kernel,
        in_specs=[anywhere] * 4,
        out_shape=jax.ShapeDtypeStruct((devices * SENT_ROWS, LANES), F32),
        scratch_shapes=[
            pltpu.VMEM((9, ROWS, LANES), F32),
            pltpu.VMEM(points.shape, F32),
            pltpu.VMEM((ROWS, LANES), jnp.int32),
            pltpu.VMEM((ROWS, LANES), jnp.int32),
            pltpu.VMEM(poses.shape, F32),
            pltpu.SemaphoreType.DMA((chunks,)),
            pltpu.SemaphoreType.DMA((3,)),
        ],
        compiler_params=pltpu.CompilerParams(vmem_limit_bytes=56 * 1024 * 1024),
    )(points, voxel_ids.reshape(ROWS, LANES), scan_ids.reshape(ROWS, LANES), poses)
    recv = lax.all_to_all(sent.reshape(devices, 1, SENT_ROWS * LANES), axes, 0, 0, tiled=True)
    recv = recv.reshape(devices * SENT_ROWS, LANES)
    shares, cost = pl.pallas_call(
        owner_kernel,
        out_shape=(
            jax.ShapeDtypeStruct((devices, 8, LANES), F32),
            jax.ShapeDtypeStruct((1, VOX), F32),
        ),
        scratch_shapes=[
            pltpu.VMEM((ROWS * 16, LANES), F32),
            pltpu.VMEM((ROWS * 16, LANES), F32),
            pltpu.VMEM((TM, SCAN_ROW, 512), BF16),
            pltpu.VMEM((VOX, 4096), BF16),
            pltpu.VMEM((ROWS * 32, LANES), F32),
        ],
        compiler_params=pltpu.CompilerParams(vmem_limit_bytes=32 * 1024 * 1024),
    )(recv, normal_angles)
    arrived = lax.all_to_all(shares, axes, 0, 0, tiled=True)
    all_scans = poses.shape[1] * devices
    scale = all_scans / (blocks * devices * PTS)
    hess, grad = pl.pallas_call(
        functools.partial(scans_kernel, scale),
        out_shape=(
            jax.ShapeDtypeStruct((SLOTS, 36), F32),
            jax.ShapeDtypeStruct((6, SLOTS), F32),
        ),
        compiler_params=pltpu.CompilerParams(vmem_limit_bytes=8 * 1024 * 1024),
    )(arrived)
    return hess.T, grad, cost.reshape(VOX)


def solution(mesh):
    return jax.shard_map(
        local,
        mesh=mesh,
        in_specs=(
            P(None, ("tm", "map"), None),
            P(None, ("tm", "map")),
            P(None, ("tm", "map")),
            P(("tm", "map")),
            P(("tm", "map")),
        ),
        out_specs=(P(None, ("tm", "map")), P(None, ("tm", "map")), P(("tm", "map"))),
        check_vma=False,
    )
```

```python
import functools

import jax
import jax.numpy as jnp
from jax import lax
from jax.experimental import pallas as pl
from jax.experimental.pallas import tpu as pltpu
from jax.sharding import PartitionSpec as P

LANES = 128
GROUPS = 4
SLOTS = 32
PTS = 128
SENT_ROWS = 5
BACK_ROWS = 7
ROWS = 32
TM = 8
SCAN_ROW = 512
VOX = 256
BF16 = jnp.bfloat16
F32 = jnp.float32


def swap_groups(rows):
    lane = lax.broadcasted_iota(jnp.int32, rows[0].shape, 1) // SLOTS
    out = []
    for g in range(GROUPS):
        acc = None
        for h in range(GROUPS):
            shift = (h - g) * SLOTS % LANES
            part = rows[h] if shift == 0 else pltpu.roll(rows[h], shift, 1)
            acc = part if acc is None else jnp.where(lane == h, part, acc)
        out.append(acc)
    return out


def split3(x):
    hi = x.astype(BF16)
    rest = x - hi.astype(F32)
    mid = rest.astype(BF16)
    lo = (rest - mid.astype(F32)).astype(BF16)
    return jnp.concatenate([hi, mid, lo], axis=0)


def fold3(x):
    n = x.shape[0] // 3
    return x[:n] + x[n : 2 * n] + x[2 * n :]


def moments_kernel(points_hbm, vox_hbm, scan_hbm, poses_hbm, sent_ref, acc_ref, points_ref, vox_ref, scan_ref, poses_ref, sems, small_sems):
    chunks = sems.shape[0]
    size = points_ref.shape[1] // chunks

    def fetch(c):
        span = pl.ds(c * size, size)
        return pltpu.make_async_copy(points_hbm.at[:, span, :], points_ref.at[:, span, :], sems.at[c])

    small = [
        pltpu.make_async_copy(vox_hbm, vox_ref, small_sems.at[0]),
        pltpu.make_async_copy(scan_hbm, scan_ref, small_sems.at[1]),
        pltpu.make_async_copy(poses_hbm, poses_ref, small_sems.at[2]),
    ]
    for c in range(chunks):
        fetch(c).start()
    for copy in small:
        copy.start()

    @pl.loop(0, chunks)
    def _(c):
        fetch(c).wait()
        for cc in range(size // LANES):
            span = pl.ds(pl.multiple_of(c * size + cc * LANES, LANES), LANES)
            x = points_ref[0, span, :].T
            y = points_ref[1, span, :].T
            z = points_ref[2, span, :].T
            quantities = [x, y, z, x * x, y * y, z * z, x * y, x * z, y * z]
            for f, q in enumerate(quantities):
                acc_ref[f, pl.ds(c * (size // LANES) + cc, 1), :] = jnp.sum(q, axis=0, keepdims=True)

    for copy in small:
        copy.wait()
    lane = lax.broadcasted_iota(jnp.int32, (ROWS, LANES), 1)
    row = lax.broadcasted_iota(jnp.int32, (ROWS, LANES), 0)
    vox = vox_ref[...]
    owner = row * GROUPS + lane // SLOTS
    vox = jnp.where(vox >= 0, vox - owner * VOX, -1).astype(F32)
    scan = scan_ref[...].astype(F32)
    p = poses_ref[...]
    p = jnp.concatenate([p, p, p, p], axis=1)
    cos, sin = jnp.cos(p[:3]), jnp.sin(p[:3])
    one = [cos[0:1], sin[0:1], cos[1:2], sin[1:2], cos[2:3], sin[2:3], p[3:4], p[4:5], p[5:6]]
    group = lax.broadcasted_iota(jnp.int32, (1, LANES), 1) // SLOTS
    f = [acc_ref[i] for i in range(9)]
    whole = lambda r: jnp.broadcast_to(r, (ROWS, LANES))
    k0 = swap_groups(f[0:4])
    k1 = swap_groups(f[4:8])
    k2 = swap_groups([f[8], vox, scan, whole(one[0])])

    def four(rs):
        r = jnp.where(group == 0, rs[0], jnp.where(group == 1, rs[1], jnp.where(group == 2, rs[2], rs[3])))
        return whole(r)

    k3 = four(one[1:5])
    k4 = four(one[5:9])
    for g in range(GROUPS):
        for k, v in enumerate([k0[g], k1[g], k2[g], k3, k4]):
            sent_ref[pl.ds(g * SENT_ROWS + k, ROWS, stride=GROUPS * SENT_ROWS), :] = v


def one_hot(condition):
    return jnp.where(condition, 1.0, 0.0).astype(BF16)


def hot16(iota, ids):
    return jnp.where(iota == ids, jnp.ones_like(iota), jnp.zeros_like(iota))


def look_up(table, index):
    low = index % LANES
    high = index // LANES
    out = None
    for k, part in enumerate(table):
        got = jnp.take_along_axis(part, low, axis=1, mode="promise_in_bounds")
        out = got if out is None else jnp.where(high == k, got, out)
    return out


def owner_kernel(recv_ref, angles_ref, out_ref, cost_ref, tab_ref, gat_ref, feat_ref):
    feats = []
    for k in range(SENT_ROWS):
        rows = [recv_ref[pl.ds(h * SENT_ROWS + k, ROWS, stride=GROUPS * SENT_ROWS), :] for h in range(GROUPS)]
        feats += swap_groups(rows)
    p1 = feats[0:3]
    pxx, pyy, pzz, pxy, pxz, pyz = feats[3:9]
    vox = feats[9].astype(jnp.int32)
    scan = feats[10].astype(jnp.int32)
    cx, sx, cy, sy, cz, sz, tx, ty, tz = feats[11:20]
    table = [
        cz * cy,
        cz * sy * sx - sz * cx,
        cz * sy * cx + sz * sx,
        sz * cy,
        sz * sy * sx + cz * cx,
        sz * sy * cx - cz * sx,
        -sy,
        cy * sx,
        cy * cx,
        tx,
        ty,
        tz,
    ]
    zeros = jnp.zeros((ROWS, LANES), F32)
    for f in range(16):
        tab_ref[pl.ds(f, ROWS, stride=16), :] = table[f] if f < 12 else zeros

    def wide(ref, t, n):
        return jnp.concatenate([ref[pl.ds((t * 4 + i) * n, n), :] for i in range(4)], axis=1)

    for t in range(TM):
        for half in range(2):
            parts = [tab_ref[pl.ds((4 * t + i) * 16 + 8 * half, 8), :] for i in range(4)]
            for i in range(4):
                r = 4 * t + i
                index = jnp.broadcast_to(scan[r : r + 1, :], (8, LANES))
                gat_ref[pl.ds(r * 16 + 8 * half, 8), :] = look_up(parts, index)

    rot = [[gat_ref[pl.ds(3 * i + j, ROWS, stride=16), :] for j in range(3)] for i in range(3)]
    tr = [gat_ref[pl.ds(9 + i, ROWS, stride=16), :] for i in range(3)]
    second = [[pxx, pxy, pxz], [pxy, pyy, pyz], [pxz, pyz, pzz]]
    rp = [sum(rot[i][j] * p1[j] for j in range(3)) for i in range(3)]
    half = [[sum(rot[i][k] * second[k][j] for k in range(3)) for j in range(3)] for i in range(3)]
    m1 = [rp[i] + PTS * tr[i] for i in range(3)]
    m2 = {}
    for i, j in [(0, 0), (1, 1), (2, 2), (0, 1), (0, 2), (1, 2)]:
        m2[i, j] = sum(half[i][k] * rot[j][k] for k in range(3)) + rp[i] * tr[j] + tr[i] * m1[j]
        m2[j, i] = m2[i, j]
    world = m1 + [m2[0, 0], m2[1, 1], m2[2, 2], m2[0, 1], m2[0, 2], m2[1, 2], jnp.ones((ROWS, LANES), F32)]
    for f in range(16):
        tab_ref[pl.ds(f, ROWS, stride=16), :] = world[f] if f < 10 else zeros

    nt = (((1,), (1,)), ((), ()))
    vox_iota = lax.broadcasted_iota(jnp.int32, (VOX, LANES), 0).astype(F32).astype(BF16)
    vox16 = vox.astype(F32).astype(BF16)
    sums = jnp.zeros((48, VOX), F32)
    for t in range(TM):
        hot = jnp.concatenate([hot16(vox_iota, vox16[r : r + 1, :]) for r in range(4 * t, 4 * t + 4)], axis=1)
        sums = sums + lax.dot_general(split3(wide(tab_ref, t, 16)), hot, nt, preferred_element_type=F32)
    sums = fold3(sums)
    count = jnp.maximum(sums[9:10] * PTS, 1.0)
    angles = angles_ref[...]
    cos, sin = jnp.cos(angles), jnp.sin(angles)
    n = [sin[0:1] * cos[1:2], sin[0:1] * sin[1:2], cos[0:1]]
    offset = (n[0] * sums[0:1] + n[1] * sums[1:2] + n[2] * sums[2:3]) / count
    quadric = (
        n[0] * n[0] * sums[3:4]
        + n[1] * n[1] * sums[4:5]
        + n[2] * n[2] * sums[5:6]
        + 2.0 * (n[0] * n[1] * sums[6:7] + n[0] * n[2] * sums[7:8] + n[1] * n[2] * sums[8:9])
    )
    cost_ref[...] = quadric / count - offset * offset
    plane = jnp.concatenate(n + [offset] + n + [offset], axis=0)
    parts = [plane[:, k * LANES : (k + 1) * LANES] for k in range(VOX // LANES)]
    sub = lax.broadcasted_iota(jnp.int32, (8, LANES), 0)
    for r in range(0, ROWS, 2):
        index = jnp.where(sub < 4, vox[r : r + 1, :], vox[r + 1 : r + 2, :])
        got = look_up(parts, jnp.maximum(index, 0))
        gat_ref[pl.ds(r * 4, 8), :] = jnp.where(index >= 0, got, 0.0)
    n0, n1, n2, d = [gat_ref[pl.ds(f, ROWS, stride=4), :] for f in range(4)]
    nb = [n0, n1, n2]

    def cross(v):
        return [v[1] * n2 - v[2] * n1, v[2] * n0 - v[0] * n2, v[0] * n1 - v[1] * n0]

    am2 = list(zip(*[cross([m2[0, j], m2[1, j], m2[2, j]]) for j in range(3)]))
    ama = [cross(am2[i]) for i in range(3)]
    am1 = cross(m1)
    terms = {}
    for i in range(3):
        for j in range(i, 3):
            terms[i, j] = ama[i][j]
            terms[3 + i, 3 + j] = PTS * nb[i] * nb[j]
        for j in range(3):
            terms[i, 3 + j] = am1[i] * nb[j]
    resid = sum(nb[i] * m1[i] for i in range(3)) - PTS * d
    grad = [sum(am2[i][j] * nb[j] for j in range(3)) - d * am1[i] for i in range(3)] + [nb[i] * resid for i in range(3)]
    features = [terms[i, j] for i in range(6) for j in range(i, 6)] + grad
    for row in range(32):
        f = row % 8 * 4 + row // 8
        feat_ref[pl.ds(row, ROWS, stride=32), :] = features[f] if f < 27 else zeros

    high = [one_hot(scan >= 256) if k else one_hot(scan < 256) for k in range(2)]
    low = (scan % 256).astype(F32).T.astype(BF16)
    scan_iota = lax.broadcasted_iota(jnp.int32, (LANES, 256), 1).astype(F32).astype(BF16)
    for t in range(TM):
        ft = wide(feat_ref, t, 32)
        hi = ft.astype(BF16)
        lo = (ft - hi.astype(F32)).astype(BF16)
        both = jnp.concatenate([hi, lo], axis=0)
        masks = [jnp.concatenate([h[r : r + 1, :] for r in range(4 * t, 4 * t + 4)], axis=1) for h in high]
        left = jnp.concatenate([both * m for m in masks], axis=0)
        hot = jnp.concatenate([hot16(scan_iota, low[:, r : r + 1]) for r in range(4 * t, 4 * t + 4)], axis=0)
        got = jnp.dot(left, hot, preferred_element_type=F32)
        for c in range(4):
            top = 64 * (c // 2)
            lanes = slice(c % 2 * LANES, (c % 2 + 1) * LANES)
            sums_c = got[top : top + 32, lanes] + got[top + 32 : top + 64, lanes]
            part = [sums_c[8 * j : 8 * j + 8] for j in range(4)]
            for g, v in enumerate(swap_groups(part)):
                out_ref[pl.ds((t * 16 + 4 * c + g) * BACK_ROWS, BACK_ROWS), :] = v[:BACK_ROWS]


def scans_kernel(scale, recv_ref, hess_ref, grad_ref):
    eight = 8 * BACK_ROWS
    acc = recv_ref[0:eight, :]
    for q in range(1, recv_ref.shape[0] // eight):
        acc = acc + recv_ref[q * eight : (q + 1) * eight, :]
    total = sum(acc[q * BACK_ROWS : (q + 1) * BACK_ROWS] for q in range(8)) * scale
    part = [total[:, j * SLOTS : (j + 1) * SLOTS] for j in range(4)]
    rows = [part[f % 4][f // 4 : f // 4 + 1] for f in range(27)]
    place = {ij: f for f, ij in enumerate([(i, j) for i in range(6) for j in range(i, 6)])}
    hess = [rows[place[min(i, j), max(i, j)]] for i in range(6) for j in range(6)]
    hess_ref[...] = jnp.concatenate(hess, axis=0).T
    grad_ref[...] = jnp.concatenate(rows[21:], axis=0)


def moments(points, voxel_ids, scan_ids, poses, devices):
    anywhere = pl.BlockSpec(memory_space=pl.ANY)
    chunks = 8
    return pl.pallas_call(
        moments_kernel,
        in_specs=[anywhere] * 4,
        out_shape=jax.ShapeDtypeStruct((devices * SENT_ROWS, LANES), F32),
        scratch_shapes=[
            pltpu.VMEM((9, ROWS, LANES), F32),
            pltpu.VMEM(points.shape, F32),
            pltpu.VMEM((ROWS, LANES), jnp.int32),
            pltpu.VMEM((ROWS, LANES), jnp.int32),
            pltpu.VMEM(poses.shape, F32),
            pltpu.SemaphoreType.DMA((chunks,)),
            pltpu.SemaphoreType.DMA((3,)),
        ],
        compiler_params=pltpu.CompilerParams(vmem_limit_bytes=56 * 1024 * 1024),
    )(points, voxel_ids.reshape(ROWS, LANES), scan_ids.reshape(ROWS, LANES), poses)


def owner(recv, normal_angles, devices):
    return pl.pallas_call(
        owner_kernel,
        out_shape=(
            jax.ShapeDtypeStruct((devices * BACK_ROWS, LANES), F32),
            jax.ShapeDtypeStruct((1, VOX), F32),
        ),
        scratch_shapes=[
            pltpu.VMEM((ROWS * 16, LANES), F32),
            pltpu.VMEM((ROWS * 16, LANES), F32),
            pltpu.VMEM((ROWS * 32, LANES), F32),
        ],
        compiler_params=pltpu.CompilerParams(vmem_limit_bytes=32 * 1024 * 1024),
    )(recv, normal_angles)


def local(points, poses, normal_angles, voxel_ids, scan_ids):
    axes = ("tm", "map")
    blocks = points.shape[1]
    devices = lax.axis_size(axes)
    sent = moments(points, voxel_ids, scan_ids, poses, devices)
    recv = lax.all_to_all(sent.reshape(devices, 1, SENT_ROWS * LANES), axes, 0, 0, tiled=True)
    recv = recv.reshape(devices * SENT_ROWS, LANES)
    shares, cost = owner(recv, normal_angles, devices)
    arrived = lax.all_to_all(shares.reshape(devices, 1, BACK_ROWS * LANES), axes, 0, 0, tiled=True)
    arrived = arrived.reshape(devices * BACK_ROWS, LANES)
    all_scans = poses.shape[1] * devices
    scale = all_scans / (blocks * devices * PTS)
    hess, grad = pl.pallas_call(
        functools.partial(scans_kernel, scale),
        out_shape=(
            jax.ShapeDtypeStruct((SLOTS, 36), F32),
            jax.ShapeDtypeStruct((6, SLOTS), F32),
        ),
        compiler_params=pltpu.CompilerParams(vmem_limit_bytes=8 * 1024 * 1024),
    )(arrived)
    return hess.T, grad, cost.reshape(VOX)


def solution(mesh):
    return jax.shard_map(
        local,
        mesh=mesh,
        in_specs=(
            P(None, ("tm", "map"), None),
            P(None, ("tm", "map")),
            P(None, ("tm", "map")),
            P(("tm", "map")),
            P(("tm", "map")),
        ),
        out_specs=(P(None, ("tm", "map")), P(None, ("tm", "map")), P(("tm", "map"))),
        check_vma=False,
    )
```

```python
import functools

import jax
import jax.numpy as jnp
from jax import lax
from jax.experimental import pallas as pl
from jax.experimental.pallas import tpu as pltpu
from jax.sharding import PartitionSpec as P

LANES = 128
GROUPS = 4
SLOTS = 32
PTS = 128
SENT_ROWS = 5
BACK_ROWS = 7
ROWS = 32
TM = 8
SCAN_ROW = 512
VOX = 256
BF16 = jnp.bfloat16
F32 = jnp.float32


def swap_groups(rows):
    lane = lax.broadcasted_iota(jnp.int32, rows[0].shape, 1) // SLOTS
    out = []
    for g in range(GROUPS):
        acc = None
        for h in range(GROUPS):
            shift = (h - g) * SLOTS % LANES
            part = rows[h] if shift == 0 else pltpu.roll(rows[h], shift, 1)
            acc = part if acc is None else jnp.where(lane == h, part, acc)
        out.append(acc)
    return out


def split3(x):
    hi = x.astype(BF16)
    rest = x - hi.astype(F32)
    mid = rest.astype(BF16)
    lo = (rest - mid.astype(F32)).astype(BF16)
    return jnp.concatenate([hi, mid, lo], axis=0)


def fold3(x):
    n = x.shape[0] // 3
    return x[:n] + x[n : 2 * n] + x[2 * n :]


def moments_kernel(points_hbm, vox_hbm, scan_hbm, poses_hbm, sent_ref, acc_ref, points_ref, vox_ref, scan_ref, poses_ref, sems, small_sems):
    chunks = sems.shape[0]
    size = points_ref.shape[1] // chunks

    def fetch(c):
        span = pl.ds(c * size, size)
        return pltpu.make_async_copy(points_hbm.at[:, span, :], points_ref.at[:, span, :], sems.at[c])

    small = [
        pltpu.make_async_copy(vox_hbm, vox_ref, small_sems.at[0]),
        pltpu.make_async_copy(scan_hbm, scan_ref, small_sems.at[1]),
        pltpu.make_async_copy(poses_hbm, poses_ref, small_sems.at[2]),
    ]
    for c in range(chunks):
        fetch(c).start()
    for copy in small:
        copy.start()

    @pl.loop(0, chunks)
    def _(c):
        fetch(c).wait()
        for cc in range(size // LANES):
            span = pl.ds(pl.multiple_of(c * size + cc * LANES, LANES), LANES)
            x = points_ref[0, span, :].T
            y = points_ref[1, span, :].T
            z = points_ref[2, span, :].T
            quantities = [x, y, z, x * x, y * y, z * z, x * y, x * z, y * z]
            for f, q in enumerate(quantities):
                acc_ref[f, pl.ds(c * (size // LANES) + cc, 1), :] = jnp.sum(q, axis=0, keepdims=True)

    for copy in small:
        copy.wait()
    lane = lax.broadcasted_iota(jnp.int32, (ROWS, LANES), 1)
    row = lax.broadcasted_iota(jnp.int32, (ROWS, LANES), 0)
    vox = vox_ref[...]
    owner = row * GROUPS + lane // SLOTS
    vox = jnp.where(vox >= 0, vox - owner * VOX, -1).astype(F32)
    scan = scan_ref[...].astype(F32)
    p = poses_ref[...]
    p = jnp.concatenate([p, p, p, p], axis=1)
    half = 0.5 * p[:3]
    tangent = jnp.sin(half) / jnp.cos(half)
    one = [tangent[0:1], tangent[1:2], tangent[2:3], p[3:4], p[4:5], p[5:6]]
    group = lax.broadcasted_iota(jnp.int32, (1, LANES), 1) // SLOTS
    f = [acc_ref[i] for i in range(9)]
    whole = lambda r: jnp.broadcast_to(r, (ROWS, LANES))
    k0 = swap_groups(f[0:4])
    k1 = swap_groups(f[4:8])
    k2 = swap_groups([f[8], vox, scan, whole(one[0])])

    def four(rs):
        r = jnp.where(group == 0, rs[0], jnp.where(group == 1, rs[1], jnp.where(group == 2, rs[2], rs[3])))
        return whole(r)

    k3 = four(one[1:5])
    k4 = whole(jnp.where(group == 0, one[5], 0.0))
    for g in range(GROUPS):
        for k, v in enumerate([k0[g], k1[g], k2[g], k3, k4]):
            sent_ref[pl.ds(g * SENT_ROWS + k, ROWS, stride=GROUPS * SENT_ROWS), :] = v


def one_hot(condition):
    return jnp.where(condition, 1.0, 0.0).astype(BF16)


def hot16(iota, ids):
    return jnp.where(iota == ids, jnp.ones_like(iota), jnp.zeros_like(iota))


def look_up(table, index):
    low = index % LANES
    high = index // LANES
    out = None
    for k, part in enumerate(table):
        got = jnp.take_along_axis(part, low, axis=1, mode="promise_in_bounds")
        out = got if out is None else jnp.where(high == k, got, out)
    return out


def owner_kernel(recv_ref, angles_ref, out_ref, cost_ref, tab_ref, gat_ref, feat_ref):
    feats = []
    for k in range(SENT_ROWS):
        rows = [recv_ref[pl.ds(h * SENT_ROWS + k, ROWS, stride=GROUPS * SENT_ROWS), :] for h in range(GROUPS)]
        feats += swap_groups(rows)
    p1 = feats[0:3]
    pxx, pyy, pzz, pxy, pxz, pyz = feats[3:9]
    vox = feats[9].astype(jnp.int32)
    scan = feats[10].astype(jnp.int32)
    zeros = jnp.zeros((ROWS, LANES), F32)
    for f in range(8):
        tab_ref[pl.ds(f, ROWS, stride=8), :] = feats[11 + f] if f < 6 else zeros

    def wide(ref, t, n):
        return jnp.concatenate([ref[pl.ds((t * 4 + i) * n, n), :] for i in range(4)], axis=1)

    scan_low = scan % LANES
    scan_bits = [scan & LANES, scan & (2 * LANES)]
    for t in range(TM):
        parts = [tab_ref[pl.ds((4 * t + i) * 8, 8), :] for i in range(4)]
        for r in range(4 * t, 4 * t + 4):
            low_index = jnp.broadcast_to(scan_low[r : r + 1, :], (8, LANES))
            got = [jnp.take_along_axis(p, low_index, axis=1, mode="promise_in_bounds") for p in parts]
            b0, b1 = [jnp.broadcast_to(b[r : r + 1, :], (8, LANES)) != 0 for b in scan_bits]
            gat_ref[pl.ds(r * 8, 8), :] = jnp.where(b1, jnp.where(b0, got[3], got[2]), jnp.where(b0, got[1], got[0]))
    pose = [gat_ref[pl.ds(f, ROWS, stride=8), :] for f in range(6)]
    inverse = [1.0 / (1.0 + u * u) for u in pose[:3]]
    sx, sy, sz = [2.0 * u * v for u, v in zip(pose[:3], inverse)]
    cx, cy, cz = [(1.0 - u * u) * v for u, v in zip(pose[:3], inverse)]
    tr = pose[3:]
    rot = [
        [cz * cy, cz * sy * sx - sz * cx, cz * sy * cx + sz * sx],
        [sz * cy, sz * sy * sx + cz * cx, sz * sy * cx - cz * sx],
        [-sy, cy * sx, cy * cx],
    ]
    second = [[pxx, pxy, pxz], [pxy, pyy, pyz], [pxz, pyz, pzz]]
    rp = [sum(rot[i][j] * p1[j] for j in range(3)) for i in range(3)]
    half = [[sum(rot[i][k] * second[k][j] for k in range(3)) for j in range(3)] for i in range(3)]
    m1 = [rp[i] + PTS * tr[i] for i in range(3)]
    m2 = {}
    for i, j in [(0, 0), (1, 1), (2, 2), (0, 1), (0, 2), (1, 2)]:
        m2[i, j] = sum(half[i][k] * rot[j][k] for k in range(3)) + rp[i] * tr[j] + tr[i] * m1[j]
        m2[j, i] = m2[i, j]
    world = m1 + [m2[0, 0], m2[1, 1], m2[2, 2], m2[0, 1], m2[0, 2], m2[1, 2], jnp.ones((ROWS, LANES), F32)]
    for f in range(16):
        tab_ref[pl.ds(f, ROWS, stride=16), :] = world[f] if f < 10 else zeros

    nt = (((1,), (1,)), ((), ()))
    vox_iota = lax.broadcasted_iota(jnp.int32, (LANES, LANES), 0).astype(F32).astype(BF16)
    vox16 = jnp.where(vox < 0, -1, vox % LANES).astype(F32).astype(BF16)
    vhigh = [one_hot(vox < LANES), one_hot(vox >= LANES)]
    sums = jnp.zeros((96, LANES), F32)
    for t in range(TM):
        hot = jnp.concatenate([hot16(vox_iota, vox16[r : r + 1, :]) for r in range(4 * t, 4 * t + 4)], axis=1)
        w = split3(wide(tab_ref, t, 16))
        masks = [jnp.concatenate([h[r : r + 1, :] for r in range(4 * t, 4 * t + 4)], axis=1) for h in vhigh]
        left = jnp.concatenate([w * m for m in masks], axis=0)
        sums = sums + lax.dot_general(left, hot, nt, preferred_element_type=F32)
    sums = jnp.concatenate([sums[:48], sums[48:]], axis=1)
    sums = fold3(sums)
    count = jnp.maximum(sums[9:10] * PTS, 1.0)
    angles = angles_ref[...]
    cos, sin = jnp.cos(angles), jnp.sin(angles)
    n = [sin[0:1] * cos[1:2], sin[0:1] * sin[1:2], cos[0:1]]
    offset = (n[0] * sums[0:1] + n[1] * sums[1:2] + n[2] * sums[2:3]) / count
    quadric = (
        n[0] * n[0] * sums[3:4]
        + n[1] * n[1] * sums[4:5]
        + n[2] * n[2] * sums[5:6]
        + 2.0 * (n[0] * n[1] * sums[6:7] + n[0] * n[2] * sums[7:8] + n[1] * n[2] * sums[8:9])
    )
    cost_ref[...] = quadric / count - offset * offset
    plane = jnp.concatenate(n + [offset] + n + [offset], axis=0)
    parts = [plane[:, k * LANES : (k + 1) * LANES] for k in range(VOX // LANES)]
    sub = lax.broadcasted_iota(jnp.int32, (8, LANES), 0)
    for r in range(0, ROWS, 2):
        index = jnp.where(sub < 4, vox[r : r + 1, :], vox[r + 1 : r + 2, :])
        got = look_up(parts, jnp.maximum(index, 0))
        gat_ref[pl.ds(r * 4, 8), :] = jnp.where(index >= 0, got, 0.0)
    n0, n1, n2, d = [gat_ref[pl.ds(f, ROWS, stride=4), :] for f in range(4)]
    nb = [n0, n1, n2]

    def cross(v):
        return [v[1] * n2 - v[2] * n1, v[2] * n0 - v[0] * n2, v[0] * n1 - v[1] * n0]

    am2 = list(zip(*[cross([m2[0, j], m2[1, j], m2[2, j]]) for j in range(3)]))
    ama = [cross(am2[i]) for i in range(3)]
    am1 = cross(m1)
    terms = {}
    for i in range(3):
        for j in range(i, 3):
            terms[i, j] = ama[i][j]
            terms[3 + i, 3 + j] = PTS * nb[i] * nb[j]
        for j in range(3):
            terms[i, 3 + j] = am1[i] * nb[j]
    resid = sum(nb[i] * m1[i] for i in range(3)) - PTS * d
    grad = [sum(am2[i][j] * nb[j] for j in range(3)) - d * am1[i] for i in range(3)] + [nb[i] * resid for i in range(3)]
    features = [terms[i, j] for i in range(6) for j in range(i, 6)] + grad
    for row in range(32):
        f = row % 8 * 4 + row // 8
        feat_ref[pl.ds(row, ROWS, stride=32), :] = features[f] if f < 27 else zeros

    high = [one_hot(scan >= 256) if k else one_hot(scan < 256) for k in range(2)]
    low = (scan % 256).astype(F32).T.astype(BF16)
    scan_iota = lax.broadcasted_iota(jnp.int32, (LANES, 256), 1).astype(F32).astype(BF16)
    for t in range(TM):
        ft = wide(feat_ref, t, 32)
        hi = ft.astype(BF16)
        lo = (ft - hi.astype(F32)).astype(BF16)
        both = jnp.concatenate([hi, lo], axis=0)
        masks = [jnp.concatenate([h[r : r + 1, :] for r in range(4 * t, 4 * t + 4)], axis=1) for h in high]
        left = jnp.concatenate([both * m for m in masks], axis=0)
        hot = jnp.concatenate([hot16(scan_iota, low[:, r : r + 1]) for r in range(4 * t, 4 * t + 4)], axis=0)
        got = jnp.dot(left, hot, preferred_element_type=F32)
        for c in range(4):
            top = 64 * (c // 2)
            lanes = slice(c % 2 * LANES, (c % 2 + 1) * LANES)
            sums_c = got[top : top + 32, lanes] + got[top + 32 : top + 64, lanes]
            part = [sums_c[8 * j : 8 * j + 8] for j in range(4)]
            for g, v in enumerate(swap_groups(part)):
                out_ref[pl.ds((t * 16 + 4 * c + g) * BACK_ROWS, BACK_ROWS), :] = v[:BACK_ROWS]


def scans_kernel(scale, recv_ref, hess_ref, grad_ref):
    eight = 8 * BACK_ROWS
    acc = recv_ref[0:eight, :]
    for q in range(1, recv_ref.shape[0] // eight):
        acc = acc + recv_ref[q * eight : (q + 1) * eight, :]
    total = sum(acc[q * BACK_ROWS : (q + 1) * BACK_ROWS] for q in range(8)) * scale
    part = [total[:, j * SLOTS : (j + 1) * SLOTS] for j in range(4)]
    rows = [part[f % 4][f // 4 : f // 4 + 1] for f in range(27)]
    place = {ij: f for f, ij in enumerate([(i, j) for i in range(6) for j in range(i, 6)])}
    hess = [rows[place[min(i, j), max(i, j)]] for i in range(6) for j in range(6)]
    hess_ref[...] = jnp.concatenate(hess, axis=0).T
    grad_ref[...] = jnp.concatenate(rows[21:], axis=0)


def moments(points, voxel_ids, scan_ids, poses, devices):
    anywhere = pl.BlockSpec(memory_space=pl.ANY)
    chunks = 8
    return pl.pallas_call(
        moments_kernel,
        in_specs=[anywhere] * 4,
        out_shape=jax.ShapeDtypeStruct((devices * SENT_ROWS, LANES), F32),
        scratch_shapes=[
            pltpu.VMEM((9, ROWS, LANES), F32),
            pltpu.VMEM(points.shape, F32),
            pltpu.VMEM((ROWS, LANES), jnp.int32),
            pltpu.VMEM((ROWS, LANES), jnp.int32),
            pltpu.VMEM(poses.shape, F32),
            pltpu.SemaphoreType.DMA((chunks,)),
            pltpu.SemaphoreType.DMA((3,)),
        ],
        compiler_params=pltpu.CompilerParams(vmem_limit_bytes=56 * 1024 * 1024),
    )(points, voxel_ids.reshape(ROWS, LANES), scan_ids.reshape(ROWS, LANES), poses)


def owner(recv, normal_angles, devices):
    return pl.pallas_call(
        owner_kernel,
        out_shape=(
            jax.ShapeDtypeStruct((devices * BACK_ROWS, LANES), F32),
            jax.ShapeDtypeStruct((1, VOX), F32),
        ),
        scratch_shapes=[
            pltpu.VMEM((ROWS * 16, LANES), F32),
            pltpu.VMEM((ROWS * 16, LANES), F32),
            pltpu.VMEM((ROWS * 32, LANES), F32),
        ],
        compiler_params=pltpu.CompilerParams(vmem_limit_bytes=32 * 1024 * 1024),
    )(recv, normal_angles)


def local(points, poses, normal_angles, voxel_ids, scan_ids):
    axes = ("tm", "map")
    blocks = points.shape[1]
    devices = lax.axis_size(axes)
    sent = moments(points, voxel_ids, scan_ids, poses, devices)
    recv = lax.all_to_all(sent.reshape(devices, 1, SENT_ROWS * LANES), axes, 0, 0, tiled=True)
    recv = recv.reshape(devices * SENT_ROWS, LANES)
    shares, cost = owner(recv, normal_angles, devices)
    arrived = lax.all_to_all(shares.reshape(devices, 1, BACK_ROWS * LANES), axes, 0, 0, tiled=True)
    arrived = arrived.reshape(devices * BACK_ROWS, LANES)
    all_scans = poses.shape[1] * devices
    scale = all_scans / (blocks * devices * PTS)
    hess, grad = pl.pallas_call(
        functools.partial(scans_kernel, scale),
        out_shape=(
            jax.ShapeDtypeStruct((SLOTS, 36), F32),
            jax.ShapeDtypeStruct((6, SLOTS), F32),
        ),
        compiler_params=pltpu.CompilerParams(vmem_limit_bytes=8 * 1024 * 1024),
    )(arrived)
    return hess.T, grad, cost.reshape(VOX)


def solution(mesh):
    return jax.shard_map(
        local,
        mesh=mesh,
        in_specs=(
            P(None, ("tm", "map"), None),
            P(None, ("tm", "map")),
            P(None, ("tm", "map")),
            P(("tm", "map")),
            P(("tm", "map")),
        ),
        out_specs=(P(None, ("tm", "map")), P(None, ("tm", "map")), P(("tm", "map"))),
        check_vma=False,
    )
```

```python
import functools

import jax
import jax.numpy as jnp
from jax import lax
from jax.experimental import pallas as pl
from jax.experimental.pallas import tpu as pltpu
from jax.sharding import PartitionSpec as P

LANES = 128
GROUPS = 4
SLOTS = 32
PTS = 128
SENT_ROWS = 5
BACK_ROWS = 7
ROWS = 32
TM = 8
SCAN_ROW = 512
VOX = 256
BF16 = jnp.bfloat16
F32 = jnp.float32


def swap_groups(rows):
    lane = lax.broadcasted_iota(jnp.int32, rows[0].shape, 1) // SLOTS
    out = []
    for g in range(GROUPS):
        acc = None
        for h in range(GROUPS):
            shift = (h - g) * SLOTS % LANES
            part = rows[h] if shift == 0 else pltpu.roll(rows[h], shift, 1)
            acc = part if acc is None else jnp.where(lane == h, part, acc)
        out.append(acc)
    return out


def split3(x):
    hi = x.astype(BF16)
    rest = x - hi.astype(F32)
    mid = rest.astype(BF16)
    lo = (rest - mid.astype(F32)).astype(BF16)
    return jnp.concatenate([hi, mid, lo], axis=0)


def fold3(x):
    n = x.shape[0] // 3
    return x[:n] + x[n : 2 * n] + x[2 * n :]


def moments_kernel(points_hbm, vox_hbm, scan_hbm, poses_hbm, sent_ref, acc_ref, points_ref, vox_ref, scan_ref, poses_ref, sems, small_sems):
    chunks = sems.shape[0]
    size = points_ref.shape[1] // chunks

    def fetch(c):
        span = pl.ds(c * size, size)
        return pltpu.make_async_copy(points_hbm.at[:, span, :], points_ref.at[:, span, :], sems.at[c])

    small = [
        pltpu.make_async_copy(vox_hbm, vox_ref, small_sems.at[0]),
        pltpu.make_async_copy(scan_hbm, scan_ref, small_sems.at[1]),
        pltpu.make_async_copy(poses_hbm, poses_ref, small_sems.at[2]),
    ]
    for c in range(chunks):
        fetch(c).start()
    for copy in small:
        copy.start()

    @pl.loop(0, chunks)
    def _(c):
        fetch(c).wait()
        for cc in range(size // LANES):
            span = pl.ds(pl.multiple_of(c * size + cc * LANES, LANES), LANES)
            x = points_ref[0, span, :].T
            y = points_ref[1, span, :].T
            z = points_ref[2, span, :].T
            quantities = [x, y, z, x * x, y * y, z * z, x * y, x * z, y * z]
            for f, q in enumerate(quantities):
                acc_ref[f, pl.ds(c * (size // LANES) + cc, 1), :] = jnp.sum(q, axis=0, keepdims=True)

    for copy in small:
        copy.wait()
    lane = lax.broadcasted_iota(jnp.int32, (ROWS, LANES), 1)
    row = lax.broadcasted_iota(jnp.int32, (ROWS, LANES), 0)
    vox = vox_ref[...]
    owner = row * GROUPS + lane // SLOTS
    vox = jnp.where(vox >= 0, vox - owner * VOX, -1).astype(F32)
    scan = scan_ref[...].astype(F32)
    p = poses_ref[...]
    p = jnp.concatenate([p, p, p, p], axis=1)
    half = 0.5 * p[:3]
    tangent = jnp.sin(half) / jnp.cos(half)
    one = [tangent[0:1], tangent[1:2], tangent[2:3], p[3:4], p[4:5], p[5:6]]
    group = lax.broadcasted_iota(jnp.int32, (1, LANES), 1) // SLOTS
    f = [acc_ref[i] for i in range(9)]
    whole = lambda r: jnp.broadcast_to(r, (ROWS, LANES))
    k0 = swap_groups(f[0:4])
    k1 = swap_groups(f[4:8])
    k2 = swap_groups([f[8], vox, scan, whole(one[0])])

    def four(rs):
        r = jnp.where(group == 0, rs[0], jnp.where(group == 1, rs[1], jnp.where(group == 2, rs[2], rs[3])))
        return whole(r)

    k3 = four(one[1:5])
    k4 = whole(jnp.where(group == 0, one[5], 0.0))
    for g in range(GROUPS):
        for k, v in enumerate([k0[g], k1[g], k2[g], k3, k4]):
            sent_ref[pl.ds(g * SENT_ROWS + k, ROWS, stride=GROUPS * SENT_ROWS), :] = v


def one_hot(condition):
    return jnp.where(condition, 1.0, 0.0).astype(BF16)


def hot16(iota, ids):
    return jnp.where(iota == ids, jnp.ones_like(iota), jnp.zeros_like(iota))


def look_up(table, index):
    low = index % LANES
    high = index // LANES
    out = None
    for k, part in enumerate(table):
        got = jnp.take_along_axis(part, low, axis=1, mode="promise_in_bounds")
        out = got if out is None else jnp.where(high == k, got, out)
    return out


def owner_kernel(recv_ref, angles_ref, out_ref, cost_ref, tab_ref, gat_ref, feat_ref):
    feats = []
    for k in range(SENT_ROWS):
        rows = [recv_ref[pl.ds(h * SENT_ROWS + k, ROWS, stride=GROUPS * SENT_ROWS), :] for h in range(GROUPS)]
        feats += swap_groups(rows)
    p1 = feats[0:3]
    pxx, pyy, pzz, pxy, pxz, pyz = feats[3:9]
    vox = feats[9].astype(jnp.int32)
    scan = feats[10].astype(jnp.int32)
    zeros = jnp.zeros((ROWS, LANES), F32)
    for f in range(8):
        tab_ref[pl.ds(f, ROWS, stride=8), :] = feats[11 + f] if f < 6 else zeros

    def wide(ref, t, n):
        return jnp.concatenate([ref[pl.ds((t * 4 + i) * n, n), :] for i in range(4)], axis=1)

    scan_low = scan % LANES
    scan_bits = [scan & LANES, scan & (2 * LANES)]
    for t in range(TM):
        parts = [tab_ref[pl.ds((4 * t + i) * 8, 8), :] for i in range(4)]
        for r in range(4 * t, 4 * t + 4):
            low_index = jnp.broadcast_to(scan_low[r : r + 1, :], (8, LANES))
            got = [jnp.take_along_axis(p, low_index, axis=1, mode="promise_in_bounds") for p in parts]
            b0, b1 = [jnp.broadcast_to(b[r : r + 1, :], (8, LANES)) != 0 for b in scan_bits]
            gat_ref[pl.ds(r * 8, 8), :] = jnp.where(b1, jnp.where(b0, got[3], got[2]), jnp.where(b0, got[1], got[0]))
    pose = [gat_ref[pl.ds(f, ROWS, stride=8), :] for f in range(6)]
    inverse = [1.0 / (1.0 + u * u) for u in pose[:3]]
    sx, sy, sz = [2.0 * u * v for u, v in zip(pose[:3], inverse)]
    cx, cy, cz = [(1.0 - u * u) * v for u, v in zip(pose[:3], inverse)]
    tr = pose[3:]
    rot = [
        [cz * cy, cz * sy * sx - sz * cx, cz * sy * cx + sz * sx],
        [sz * cy, sz * sy * sx + cz * cx, sz * sy * cx - cz * sx],
        [-sy, cy * sx, cy * cx],
    ]
    second = [[pxx, pxy, pxz], [pxy, pyy, pyz], [pxz, pyz, pzz]]
    rp = [sum(rot[i][j] * p1[j] for j in range(3)) for i in range(3)]
    half = [[sum(rot[i][k] * second[k][j] for k in range(3)) for j in range(3)] for i in range(3)]
    m1 = [rp[i] + PTS * tr[i] for i in range(3)]
    m2 = {}
    for i, j in [(0, 0), (1, 1), (2, 2), (0, 1), (0, 2), (1, 2)]:
        m2[i, j] = sum(half[i][k] * rot[j][k] for k in range(3)) + rp[i] * tr[j] + tr[i] * m1[j]
        m2[j, i] = m2[i, j]
    world = m1 + [m2[0, 0], m2[1, 1], m2[2, 2], m2[0, 1], m2[0, 2], m2[1, 2], jnp.ones((ROWS, LANES), F32)]
    for f in range(16):
        tab_ref[pl.ds(f, ROWS, stride=16), :] = world[f] if f < 10 else zeros

    nt = (((1,), (1,)), ((), ()))
    vox_iota = lax.broadcasted_iota(jnp.int32, (LANES, LANES), 0).astype(F32).astype(BF16)
    vox16 = jnp.where(vox < 0, -1, vox % LANES).astype(F32).astype(BF16)
    vhigh = [one_hot(vox < LANES), one_hot(vox >= LANES)]
    sums = jnp.zeros((96, LANES), F32)
    for t in range(TM):
        hot = jnp.concatenate([hot16(vox_iota, vox16[r : r + 1, :]) for r in range(4 * t, 4 * t + 4)], axis=1)
        w = split3(wide(tab_ref, t, 16))
        masks = [jnp.concatenate([h[r : r + 1, :] for r in range(4 * t, 4 * t + 4)], axis=1) for h in vhigh]
        left = jnp.concatenate([w * m for m in masks], axis=0)
        sums = sums + lax.dot_general(left, hot, nt, preferred_element_type=F32)
    sums = jnp.concatenate([sums[:48], sums[48:]], axis=1)
    sums = fold3(sums)
    count = jnp.maximum(sums[9:10] * PTS, 1.0)
    angles = angles_ref[...]
    cos, sin = jnp.cos(angles), jnp.sin(angles)
    n = [sin[0:1] * cos[1:2], sin[0:1] * sin[1:2], cos[0:1]]
    offset = (n[0] * sums[0:1] + n[1] * sums[1:2] + n[2] * sums[2:3]) / count
    quadric = (
        n[0] * n[0] * sums[3:4]
        + n[1] * n[1] * sums[4:5]
        + n[2] * n[2] * sums[5:6]
        + 2.0 * (n[0] * n[1] * sums[6:7] + n[0] * n[2] * sums[7:8] + n[1] * n[2] * sums[8:9])
    )
    cost_ref[...] = quadric / count - offset * offset
    plane = jnp.concatenate(n + [offset] + n + [offset], axis=0)
    parts = [plane[:, k * LANES : (k + 1) * LANES] for k in range(VOX // LANES)]
    sub = lax.broadcasted_iota(jnp.int32, (8, LANES), 0)
    for r in range(0, ROWS, 2):
        index = jnp.where(sub < 4, vox[r : r + 1, :], vox[r + 1 : r + 2, :])
        got = look_up(parts, jnp.maximum(index, 0))
        gat_ref[pl.ds(r * 4, 8), :] = jnp.where(index >= 0, got, 0.0)
    n0, n1, n2, d = [gat_ref[pl.ds(f, ROWS, stride=4), :] for f in range(4)]
    nb = [n0, n1, n2]

    def cross(v):
        return [v[1] * n2 - v[2] * n1, v[2] * n0 - v[0] * n2, v[0] * n1 - v[1] * n0]

    am2 = list(zip(*[cross([m2[0, j], m2[1, j], m2[2, j]]) for j in range(3)]))
    ama = [cross(am2[i]) for i in range(3)]
    am1 = cross(m1)
    terms = {}
    for i in range(3):
        for j in range(i, 3):
            terms[i, j] = ama[i][j]
            terms[3 + i, 3 + j] = PTS * nb[i] * nb[j]
        for j in range(3):
            terms[i, 3 + j] = am1[i] * nb[j]
    resid = sum(nb[i] * m1[i] for i in range(3)) - PTS * d
    grad = [sum(am2[i][j] * nb[j] for j in range(3)) - d * am1[i] for i in range(3)] + [nb[i] * resid for i in range(3)]
    features = [terms[i, j] for i in range(6) for j in range(i, 6)] + grad
    for row in range(32):
        f = row % 8 * 4 + row // 8
        feat_ref[pl.ds(row, ROWS, stride=32), :] = features[f] if f < 27 else zeros

    high = [one_hot(scan >= 256) if k else one_hot(scan < 256) for k in range(2)]
    low = (scan % 256).astype(F32).T.astype(BF16)
    scan_iota = lax.broadcasted_iota(jnp.int32, (LANES, 256), 1).astype(F32).astype(BF16)
    for t in range(TM):
        ft = wide(feat_ref, t, 32)
        hi = ft.astype(BF16)
        lo = (ft - hi.astype(F32)).astype(BF16)
        both = jnp.concatenate([hi, lo], axis=0)
        masks = [jnp.concatenate([h[r : r + 1, :] for r in range(4 * t, 4 * t + 4)], axis=1) for h in high]
        left = jnp.concatenate([both * m for m in masks], axis=0)
        hot = jnp.concatenate([hot16(scan_iota, low[:, r : r + 1]) for r in range(4 * t, 4 * t + 4)], axis=0)
        got = jnp.dot(left, hot, preferred_element_type=F32)
        for c in range(4):
            top = 64 * (c // 2)
            lanes = slice(c % 2 * LANES, (c % 2 + 1) * LANES)
            sums_c = got[top : top + 32, lanes] + got[top + 32 : top + 64, lanes]
            part = [sums_c[8 * j : 8 * j + 8] for j in range(4)]
            for g, v in enumerate(swap_groups(part)):
                out_ref[pl.ds((t * 16 + 4 * c + g) * BACK_ROWS, BACK_ROWS), :] = v[:BACK_ROWS]


def scans_kernel(scale, recv_ref, hess_ref, grad_ref):
    eight = 8 * BACK_ROWS
    acc = recv_ref[0:eight, :]
    for q in range(1, recv_ref.shape[0] // eight):
        acc = acc + recv_ref[q * eight : (q + 1) * eight, :]
    total = sum(acc[q * BACK_ROWS : (q + 1) * BACK_ROWS] for q in range(8)) * scale
    part = [total[:, j * SLOTS : (j + 1) * SLOTS] for j in range(4)]
    rows = [part[f % 4][f // 4 : f // 4 + 1] for f in range(27)]
    place = {ij: f for f, ij in enumerate([(i, j) for i in range(6) for j in range(i, 6)])}
    hess = [rows[place[min(i, j), max(i, j)]] for i in range(6) for j in range(6)]
    hess_ref[...] = jnp.concatenate(hess, axis=0).T
    grad_ref[...] = jnp.concatenate(rows[21:], axis=0)


def moments(points, voxel_ids, scan_ids, poses, devices):
    anywhere = pl.BlockSpec(memory_space=pl.ANY)
    chunks = 8
    return pl.pallas_call(
        moments_kernel,
        in_specs=[anywhere] * 4,
        out_shape=pltpu.VMEM((devices * SENT_ROWS, LANES), F32),
        out_specs=pl.BlockSpec(memory_space=pltpu.VMEM),
        scratch_shapes=[
            pltpu.VMEM((9, ROWS, LANES), F32),
            pltpu.VMEM(points.shape, F32),
            pltpu.VMEM((ROWS, LANES), jnp.int32),
            pltpu.VMEM((ROWS, LANES), jnp.int32),
            pltpu.VMEM(poses.shape, F32),
            pltpu.SemaphoreType.DMA((chunks,)),
            pltpu.SemaphoreType.DMA((3,)),
        ],
        compiler_params=pltpu.CompilerParams(vmem_limit_bytes=56 * 1024 * 1024),
    )(points, voxel_ids.reshape(ROWS, LANES), scan_ids.reshape(ROWS, LANES), poses)


def owner(recv, normal_angles, devices):
    return pl.pallas_call(
        owner_kernel,
        out_shape=(
            jax.ShapeDtypeStruct((devices * BACK_ROWS, LANES), F32),
            jax.ShapeDtypeStruct((1, VOX), F32),
        ),
        scratch_shapes=[
            pltpu.VMEM((ROWS * 16, LANES), F32),
            pltpu.VMEM((ROWS * 16, LANES), F32),
            pltpu.VMEM((ROWS * 32, LANES), F32),
        ],
        compiler_params=pltpu.CompilerParams(vmem_limit_bytes=32 * 1024 * 1024),
    )(recv, normal_angles)


def local(points, poses, normal_angles, voxel_ids, scan_ids):
    axes = ("tm", "map")
    blocks = points.shape[1]
    devices = lax.axis_size(axes)
    sent = moments(points, voxel_ids, scan_ids, poses, devices)
    recv = lax.all_to_all(sent.reshape(devices, 1, SENT_ROWS * LANES), axes, 0, 0, tiled=True)
    recv = recv.reshape(devices * SENT_ROWS, LANES)
    shares, cost = owner(recv, normal_angles, devices)
    arrived = lax.all_to_all(shares.reshape(devices, 1, BACK_ROWS * LANES), axes, 0, 0, tiled=True)
    arrived = arrived.reshape(devices * BACK_ROWS, LANES)
    all_scans = poses.shape[1] * devices
    scale = all_scans / (blocks * devices * PTS)
    hess, grad = pl.pallas_call(
        functools.partial(scans_kernel, scale),
        out_shape=(
            jax.ShapeDtypeStruct((SLOTS, 36), F32),
            jax.ShapeDtypeStruct((6, SLOTS), F32),
        ),
        compiler_params=pltpu.CompilerParams(vmem_limit_bytes=8 * 1024 * 1024),
    )(arrived)
    return hess.T, grad, cost.reshape(VOX)


def solution(mesh):
    return jax.shard_map(
        local,
        mesh=mesh,
        in_specs=(
            P(None, ("tm", "map"), None),
            P(None, ("tm", "map")),
            P(None, ("tm", "map")),
            P(("tm", "map")),
            P(("tm", "map")),
        ),
        out_specs=(P(None, ("tm", "map")), P(None, ("tm", "map")), P(("tm", "map"))),
        check_vma=False,
    )
```

```python
import functools

import jax
import jax.numpy as jnp
from jax import lax
from jax.experimental import pallas as pl
from jax.experimental.pallas import tpu as pltpu
from jax.sharding import PartitionSpec as P

LANES = 128
GROUPS = 4
SLOTS = 32
PTS = 128
SENT_ROWS = 5
BACK_ROWS = 7
ROWS = 32
TM = 8
SCAN_ROW = 512
VOX = 256
BF16 = jnp.bfloat16
F32 = jnp.float32


def swap_groups(rows):
    lane = lax.broadcasted_iota(jnp.int32, rows[0].shape, 1) // SLOTS
    out = []
    for g in range(GROUPS):
        acc = None
        for h in range(GROUPS):
            shift = (h - g) * SLOTS % LANES
            part = rows[h] if shift == 0 else pltpu.roll(rows[h], shift, 1)
            acc = part if acc is None else jnp.where(lane == h, part, acc)
        out.append(acc)
    return out


def split3(x):
    hi = x.astype(BF16)
    rest = x - hi.astype(F32)
    mid = rest.astype(BF16)
    lo = (rest - mid.astype(F32)).astype(BF16)
    return jnp.concatenate([hi, mid, lo], axis=0)


def fold3(x):
    n = x.shape[0] // 3
    return x[:n] + x[n : 2 * n] + x[2 * n :]


def moments_kernel(points_hbm, vox_hbm, scan_hbm, poses_hbm, sent_ref, acc_ref, points_ref, vox_ref, scan_ref, poses_ref, sems, small_sems):
    chunks = sems.shape[0]
    size = points_ref.shape[1] // chunks

    def fetch(c):
        span = pl.ds(c * size, size)
        return pltpu.make_async_copy(points_hbm.at[:, span, :], points_ref.at[:, span, :], sems.at[c])

    small = [
        pltpu.make_async_copy(vox_hbm, vox_ref, small_sems.at[0]),
        pltpu.make_async_copy(scan_hbm, scan_ref, small_sems.at[1]),
        pltpu.make_async_copy(poses_hbm, poses_ref, small_sems.at[2]),
    ]
    for c in range(chunks):
        fetch(c).start()
        if c == 1:
            for copy in small:
                copy.start()

    for c in range(chunks):
        fetch(c).wait()
        for cc in range(size // LANES):
            span = pl.ds(c * size + cc * LANES, LANES)
            x = points_ref[0, span, :].T
            y = points_ref[1, span, :].T
            z = points_ref[2, span, :].T
            quantities = [x, y, z, x * x, y * y, z * z, x * y, x * z, y * z]
            for f, q in enumerate(quantities):
                acc_ref[f, pl.ds(c * (size // LANES) + cc, 1), :] = jnp.sum(q, axis=0, keepdims=True)

    for copy in small:
        copy.wait()
    lane = lax.broadcasted_iota(jnp.int32, (ROWS, LANES), 1)
    row = lax.broadcasted_iota(jnp.int32, (ROWS, LANES), 0)
    vox = vox_ref[...]
    owner = row * GROUPS + lane // SLOTS
    vox = jnp.where(vox >= 0, vox - owner * VOX, -1).astype(F32)
    scan = scan_ref[...].astype(F32)
    p = poses_ref[...]
    p = jnp.concatenate([p, p, p, p], axis=1)
    half = 0.5 * p[:3]
    tangent = jnp.sin(half) / jnp.cos(half)
    one = [tangent[0:1], tangent[1:2], tangent[2:3], p[3:4], p[4:5], p[5:6]]
    group = lax.broadcasted_iota(jnp.int32, (1, LANES), 1) // SLOTS
    f = [acc_ref[i] for i in range(9)]
    whole = lambda r: jnp.broadcast_to(r, (ROWS, LANES))
    k0 = swap_groups(f[0:4])
    k1 = swap_groups(f[4:8])
    k2 = swap_groups([f[8], vox, scan, whole(one[0])])

    def four(rs):
        r = jnp.where(group == 0, rs[0], jnp.where(group == 1, rs[1], jnp.where(group == 2, rs[2], rs[3])))
        return whole(r)

    k3 = four(one[1:5])
    k4 = whole(jnp.where(group == 0, one[5], 0.0))
    for g in range(GROUPS):
        for k, v in enumerate([k0[g], k1[g], k2[g], k3, k4]):
            sent_ref[pl.ds(g * SENT_ROWS + k, ROWS, stride=GROUPS * SENT_ROWS), :] = v


def one_hot(condition):
    return jnp.where(condition, 1.0, 0.0).astype(BF16)


def hot16(iota, ids):
    return jnp.where(iota == ids, jnp.ones_like(iota), jnp.zeros_like(iota))


def look_up(table, index):
    low = index % LANES
    high = index // LANES
    out = None
    for k, part in enumerate(table):
        got = jnp.take_along_axis(part, low, axis=1, mode="promise_in_bounds")
        out = got if out is None else jnp.where(high == k, got, out)
    return out


def owner_kernel(recv_ref, angles_ref, out_ref, cost_ref, tab_ref, gat_ref, feat_ref):
    feats = []
    for k in range(SENT_ROWS):
        rows = [recv_ref[pl.ds(h * SENT_ROWS + k, ROWS, stride=GROUPS * SENT_ROWS), :] for h in range(GROUPS)]
        if k < SENT_ROWS - 1:
            feats += swap_groups(rows)
        else:
            lane = lax.broadcasted_iota(jnp.int32, (ROWS, LANES), 1) // SLOTS
            last = rows[0]
            for h in range(1, GROUPS):
                last = jnp.where(lane == h, pltpu.roll(rows[h], h * SLOTS, 1), last)
            feats.append(last)
    p1 = feats[0:3]
    pxx, pyy, pzz, pxy, pxz, pyz = feats[3:9]
    vox = feats[9].astype(jnp.int32)
    scan = feats[10].astype(jnp.int32)
    zeros = jnp.zeros((ROWS, LANES), F32)
    for f in range(6):
        tab_ref[pl.ds(f, ROWS, stride=8), :] = feats[11 + f]

    def wide(ref, t, n):
        return jnp.concatenate([ref[pl.ds((t * 4 + i) * n, n), :] for i in range(4)], axis=1)

    scan_low = scan % LANES
    scan_bits = [scan & LANES, scan & (2 * LANES)]
    for t in range(TM):
        parts = [tab_ref[pl.ds((4 * t + i) * 8, 8), :] for i in range(4)]
        for r in range(4 * t, 4 * t + 4):
            low_index = jnp.broadcast_to(scan_low[r : r + 1, :], (8, LANES))
            got = [jnp.take_along_axis(p, low_index, axis=1, mode="promise_in_bounds") for p in parts]
            b0, b1 = [jnp.broadcast_to(b[r : r + 1, :], (8, LANES)) != 0 for b in scan_bits]
            gat_ref[pl.ds(r * 8, 8), :] = jnp.where(b1, jnp.where(b0, got[3], got[2]), jnp.where(b0, got[1], got[0]))
    pose = [gat_ref[pl.ds(f, ROWS, stride=8), :] for f in range(6)]
    inverse = [1.0 / (1.0 + u * u) for u in pose[:3]]
    sx, sy, sz = [2.0 * u * v for u, v in zip(pose[:3], inverse)]
    cx, cy, cz = [(1.0 - u * u) * v for u, v in zip(pose[:3], inverse)]
    tr = pose[3:]
    rot = [
        [cz * cy, cz * sy * sx - sz * cx, cz * sy * cx + sz * sx],
        [sz * cy, sz * sy * sx + cz * cx, sz * sy * cx - cz * sx],
        [-sy, cy * sx, cy * cx],
    ]
    second = [[pxx, pxy, pxz], [pxy, pyy, pyz], [pxz, pyz, pzz]]
    rp = [sum(rot[i][j] * p1[j] for j in range(3)) for i in range(3)]
    half = [[sum(rot[i][k] * second[k][j] for k in range(3)) for j in range(3)] for i in range(3)]
    m1 = [rp[i] + PTS * tr[i] for i in range(3)]
    m2 = {}
    for i, j in [(0, 0), (1, 1), (2, 2), (0, 1), (0, 2), (1, 2)]:
        m2[i, j] = sum(half[i][k] * rot[j][k] for k in range(3)) + rp[i] * tr[j] + tr[i] * m1[j]
        m2[j, i] = m2[i, j]
    world = m1 + [m2[0, 0], m2[1, 1], m2[2, 2], m2[0, 1], m2[0, 2], m2[1, 2], jnp.ones((ROWS, LANES), F32)]
    for f in range(10):
        tab_ref[pl.ds(f, ROWS, stride=16), :] = world[f]

    nt = (((1,), (1,)), ((), ()))
    vox_iota = lax.broadcasted_iota(jnp.int32, (LANES, LANES), 0).astype(F32).astype(BF16)
    vox16 = jnp.where(vox < 0, -1, vox % LANES).astype(F32).astype(BF16)
    vhigh = [one_hot(vox < LANES), one_hot(vox >= LANES)]
    sums = jnp.zeros((96, LANES), F32)
    for t in range(TM):
        hot = jnp.concatenate([hot16(vox_iota, vox16[r : r + 1, :]) for r in range(4 * t, 4 * t + 4)], axis=1)
        w = split3(wide(tab_ref, t, 16))
        masks = [jnp.concatenate([h[r : r + 1, :] for r in range(4 * t, 4 * t + 4)], axis=1) for h in vhigh]
        left = jnp.concatenate([w * m for m in masks], axis=0)
        sums = sums + lax.dot_general(left, hot, nt, preferred_element_type=F32)
    sums = jnp.concatenate([sums[:48], sums[48:]], axis=1)
    sums = fold3(sums)
    count = jnp.maximum(sums[9:10] * PTS, 1.0)
    angles = angles_ref[...]
    cos, sin = jnp.cos(angles), jnp.sin(angles)
    n = [sin[0:1] * cos[1:2], sin[0:1] * sin[1:2], cos[0:1]]
    offset = (n[0] * sums[0:1] + n[1] * sums[1:2] + n[2] * sums[2:3]) / count
    quadric = (
        n[0] * n[0] * sums[3:4]
        + n[1] * n[1] * sums[4:5]
        + n[2] * n[2] * sums[5:6]
        + 2.0 * (n[0] * n[1] * sums[6:7] + n[0] * n[2] * sums[7:8] + n[1] * n[2] * sums[8:9])
    )
    cost_ref[...] = quadric / count - offset * offset
    plane = jnp.concatenate(n + [offset] + n + [offset], axis=0)
    parts = [plane[:, k * LANES : (k + 1) * LANES] for k in range(VOX // LANES)]
    sub = lax.broadcasted_iota(jnp.int32, (8, LANES), 0)
    for r in range(0, ROWS, 2):
        index = jnp.where(sub < 4, vox[r : r + 1, :], vox[r + 1 : r + 2, :])
        got = look_up(parts, jnp.maximum(index, 0))
        gat_ref[pl.ds(r * 4, 8), :] = jnp.where(index >= 0, got, 0.0)
    n0, n1, n2, d = [gat_ref[pl.ds(f, ROWS, stride=4), :] for f in range(4)]
    nb = [n0, n1, n2]

    def cross(v):
        return [v[1] * n2 - v[2] * n1, v[2] * n0 - v[0] * n2, v[0] * n1 - v[1] * n0]

    am2 = list(zip(*[cross([m2[0, j], m2[1, j], m2[2, j]]) for j in range(3)]))
    ama = [cross(am2[i]) for i in range(3)]
    am1 = cross(m1)
    terms = {}
    for i in range(3):
        for j in range(i, 3):
            terms[i, j] = ama[i][j]
            terms[3 + i, 3 + j] = PTS * nb[i] * nb[j]
        for j in range(3):
            terms[i, 3 + j] = am1[i] * nb[j]
    resid = sum(nb[i] * m1[i] for i in range(3)) - PTS * d
    grad = [sum(am2[i][j] * nb[j] for j in range(3)) - d * am1[i] for i in range(3)] + [nb[i] * resid for i in range(3)]
    features = [terms[i, j] for i in range(6) for j in range(i, 6)] + grad
    for row in range(32):
        f = row % 8 * 4 + row // 8
        if f < 28:
            feat_ref[pl.ds(row, ROWS, stride=32), :] = features[f] if f < 27 else zeros

    high = [one_hot(scan >= 256) if k else one_hot(scan < 256) for k in range(2)]
    low = (scan % 256).astype(F32).T.astype(BF16)
    scan_iota = lax.broadcasted_iota(jnp.int32, (LANES, 256), 1).astype(F32).astype(BF16)
    for t in range(TM):
        ft = wide(feat_ref, t, 32)
        hi = ft.astype(BF16)
        lo = (ft - hi.astype(F32)).astype(BF16)
        both = jnp.concatenate([hi, lo], axis=0)
        masks = [jnp.concatenate([h[r : r + 1, :] for r in range(4 * t, 4 * t + 4)], axis=1) for h in high]
        left = jnp.concatenate([both * m for m in masks], axis=0)
        hot = jnp.concatenate([hot16(scan_iota, low[:, r : r + 1]) for r in range(4 * t, 4 * t + 4)], axis=0)
        got = jnp.dot(left, hot, preferred_element_type=F32)
        for c in range(4):
            top = 64 * (c // 2)
            lanes = slice(c % 2 * LANES, (c % 2 + 1) * LANES)
            sums_c = got[top : top + 32, lanes] + got[top + 32 : top + 64, lanes]
            part = [sums_c[8 * j : 8 * j + 8] for j in range(4)]
            for g, v in enumerate(swap_groups(part)):
                out_ref[pl.ds((t * 16 + 4 * c + g) * BACK_ROWS, BACK_ROWS), :] = v[:BACK_ROWS]


def scans_kernel(scale, recv_ref, hess_ref, grad_ref):
    eight = 8 * BACK_ROWS
    acc = recv_ref[0:eight, :]
    for q in range(1, recv_ref.shape[0] // eight):
        acc = acc + recv_ref[q * eight : (q + 1) * eight, :]
    total = sum(acc[q * BACK_ROWS : (q + 1) * BACK_ROWS] for q in range(8)) * scale
    part = [total[:, j * SLOTS : (j + 1) * SLOTS] for j in range(4)]
    rows = [part[f % 4][f // 4 : f // 4 + 1] for f in range(27)]
    place = {ij: f for f, ij in enumerate([(i, j) for i in range(6) for j in range(i, 6)])}
    hess = [rows[place[min(i, j), max(i, j)]] for i in range(6) for j in range(6)]
    hess_ref[...] = jnp.concatenate(hess, axis=0).T
    grad_ref[...] = jnp.concatenate(rows[21:], axis=0)


def moments(points, voxel_ids, scan_ids, poses, devices):
    anywhere = pl.BlockSpec(memory_space=pl.ANY)
    chunks = 4
    return pl.pallas_call(
        moments_kernel,
        in_specs=[anywhere] * 4,
        out_shape=pltpu.VMEM((devices * SENT_ROWS, LANES), F32),
        out_specs=pl.BlockSpec(memory_space=pltpu.VMEM),
        scratch_shapes=[
            pltpu.VMEM((9, ROWS, LANES), F32),
            pltpu.VMEM(points.shape, F32),
            pltpu.VMEM((ROWS, LANES), jnp.int32),
            pltpu.VMEM((ROWS, LANES), jnp.int32),
            pltpu.VMEM(poses.shape, F32),
            pltpu.SemaphoreType.DMA((chunks,)),
            pltpu.SemaphoreType.DMA((3,)),
        ],
        compiler_params=pltpu.CompilerParams(vmem_limit_bytes=56 * 1024 * 1024),
    )(points, voxel_ids.reshape(ROWS, LANES), scan_ids.reshape(ROWS, LANES), poses)


def owner(recv, normal_angles, devices):
    return pl.pallas_call(
        owner_kernel,
        out_shape=(
            jax.ShapeDtypeStruct((devices * BACK_ROWS, LANES), F32),
            jax.ShapeDtypeStruct((1, VOX), F32),
        ),
        scratch_shapes=[
            pltpu.VMEM((ROWS * 16, LANES), F32),
            pltpu.VMEM((ROWS * 16, LANES), F32),
            pltpu.VMEM((ROWS * 32, LANES), F32),
        ],
        compiler_params=pltpu.CompilerParams(vmem_limit_bytes=32 * 1024 * 1024),
    )(recv, normal_angles)


def local(points, poses, normal_angles, voxel_ids, scan_ids):
    axes = ("tm", "map")
    blocks = points.shape[1]
    devices = lax.axis_size(axes)
    sent = moments(points, voxel_ids, scan_ids, poses, devices)
    recv = lax.all_to_all(sent.reshape(devices, 1, SENT_ROWS * LANES), axes, 0, 0, tiled=True)
    recv = recv.reshape(devices * SENT_ROWS, LANES)
    shares, cost = owner(recv, normal_angles, devices)
    arrived = lax.all_to_all(shares.reshape(devices, 1, BACK_ROWS * LANES), axes, 0, 0, tiled=True)
    arrived = arrived.reshape(devices * BACK_ROWS, LANES)
    all_scans = poses.shape[1] * devices
    scale = all_scans / (blocks * devices * PTS)
    hess, grad = pl.pallas_call(
        functools.partial(scans_kernel, scale),
        out_shape=(
            jax.ShapeDtypeStruct((SLOTS, 36), F32),
            jax.ShapeDtypeStruct((6, SLOTS), F32),
        ),
        compiler_params=pltpu.CompilerParams(vmem_limit_bytes=8 * 1024 * 1024),
    )(arrived)
    return hess.T, grad, cost.reshape(VOX)


def solution(mesh):
    return jax.shard_map(
        local,
        mesh=mesh,
        in_specs=(
            P(None, ("tm", "map"), None),
            P(None, ("tm", "map")),
            P(None, ("tm", "map")),
            P(("tm", "map")),
            P(("tm", "map")),
        ),
        out_specs=(P(None, ("tm", "map")), P(None, ("tm", "map")), P(("tm", "map"))),
        check_vma=False,
    )
```

```python
import functools

import jax
import jax.numpy as jnp
from jax import lax
from jax.experimental import pallas as pl
from jax.experimental.pallas import tpu as pltpu
from jax.sharding import PartitionSpec as P

LANES = 128
GROUPS = 4
SLOTS = 32
PTS = 128
SENT_ROWS = 5
BACK_ROWS = 7
ROWS = 32
TM = 8
SCAN_ROW = 512
VOX = 256
BF16 = jnp.bfloat16
F32 = jnp.float32


def swap_groups(rows):
    lane = lax.broadcasted_iota(jnp.int32, rows[0].shape, 1) // SLOTS
    out = []
    for g in range(GROUPS):
        acc = None
        for h in range(GROUPS):
            shift = (h - g) * SLOTS % LANES
            part = rows[h] if shift == 0 else pltpu.roll(rows[h], shift, 1)
            acc = part if acc is None else jnp.where(lane == h, part, acc)
        out.append(acc)
    return out


def split3(x):
    hi = x.astype(BF16)
    rest = x - hi.astype(F32)
    mid = rest.astype(BF16)
    lo = (rest - mid.astype(F32)).astype(BF16)
    return jnp.concatenate([hi, mid, lo], axis=0)


def fold3(x):
    n = x.shape[0] // 3
    return x[:n] + x[n : 2 * n] + x[2 * n :]


def moments_kernel(points_hbm, vox_hbm, scan_hbm, poses_hbm, sent_ref, acc_ref, points_ref, vox_ref, scan_ref, poses_ref, sems, small_sems):
    chunks = sems.shape[0]
    size = points_ref.shape[1] // chunks

    def fetch(c):
        span = pl.ds(c * size, size)
        return pltpu.make_async_copy(points_hbm.at[:, span, :], points_ref.at[:, span, :], sems.at[c])

    small = [
        pltpu.make_async_copy(vox_hbm, vox_ref, small_sems.at[0]),
        pltpu.make_async_copy(scan_hbm, scan_ref, small_sems.at[1]),
        pltpu.make_async_copy(poses_hbm, poses_ref, small_sems.at[2]),
    ]
    for c in range(chunks):
        fetch(c).start()
        if c == 1:
            for copy in small:
                copy.start()

    for c in range(chunks):
        fetch(c).wait()
        for cc in range(size // LANES):
            span = pl.ds(c * size + cc * LANES, LANES)
            x = points_ref[0, span, :].T
            y = points_ref[1, span, :].T
            z = points_ref[2, span, :].T
            quantities = [x, y, z, x * x, y * y, z * z, x * y, x * z, y * z]
            for f, q in enumerate(quantities):
                acc_ref[f, pl.ds(c * (size // LANES) + cc, 1), :] = jnp.sum(q, axis=0, keepdims=True)

    for copy in small:
        copy.wait()
    lane = lax.broadcasted_iota(jnp.int32, (ROWS, LANES), 1)
    row = lax.broadcasted_iota(jnp.int32, (ROWS, LANES), 0)
    vox = vox_ref[...]
    owner = row * GROUPS + lane // SLOTS
    vox = jnp.where(vox >= 0, vox - owner * VOX, -1).astype(F32)
    scan = scan_ref[...].astype(F32)
    p = poses_ref[...]
    p = jnp.concatenate([p, p, p, p], axis=1)
    half = 0.5 * p[:3]
    tangent = jnp.sin(half) / jnp.cos(half)
    one = [tangent[0:1], tangent[1:2], tangent[2:3], p[3:4], p[4:5], p[5:6]]
    group = lax.broadcasted_iota(jnp.int32, (1, LANES), 1) // SLOTS
    f = [acc_ref[i] for i in range(9)]
    whole = lambda r: jnp.broadcast_to(r, (ROWS, LANES))
    k0 = swap_groups(f[0:4])
    k1 = swap_groups(f[4:8])
    k2 = swap_groups([f[8], vox, scan, whole(one[0])])

    def four(rs):
        r = jnp.where(group == 0, rs[0], jnp.where(group == 1, rs[1], jnp.where(group == 2, rs[2], rs[3])))
        return whole(r)

    k3 = four(one[1:5])
    k4 = whole(jnp.where(group == 0, one[5], 0.0))
    for g in range(GROUPS):
        for k, v in enumerate([k0[g], k1[g], k2[g], k3, k4]):
            sent_ref[pl.ds(g * SENT_ROWS + k, ROWS, stride=GROUPS * SENT_ROWS), :] = v


def one_hot(condition):
    return jnp.where(condition, 1.0, 0.0).astype(BF16)


def hot16(iota, ids):
    return jnp.where(iota == ids, jnp.ones_like(iota), jnp.zeros_like(iota))


def look_up(table, index):
    low = index % LANES
    high = index // LANES
    out = None
    for k, part in enumerate(table):
        got = jnp.take_along_axis(part, low, axis=1, mode="promise_in_bounds")
        out = got if out is None else jnp.where(high == k, got, out)
    return out


def owner_kernel(recv_ref, angles_ref, out_ref, cost_ref, tab_ref, gat_ref, feat_ref):
    feats = []
    for k in range(SENT_ROWS):
        rows = [recv_ref[pl.ds(h * SENT_ROWS + k, ROWS, stride=GROUPS * SENT_ROWS), :] for h in range(GROUPS)]
        if k < SENT_ROWS - 1:
            feats += swap_groups(rows)
        else:
            lane = lax.broadcasted_iota(jnp.int32, (ROWS, LANES), 1) // SLOTS
            last = rows[0]
            for h in range(1, GROUPS):
                last = jnp.where(lane == h, pltpu.roll(rows[h], h * SLOTS, 1), last)
            feats.append(last)
    p1 = feats[0:3]
    pxx, pyy, pzz, pxy, pxz, pyz = feats[3:9]
    vox = feats[9].astype(jnp.int32)
    scan = feats[10].astype(jnp.int32)
    zeros = jnp.zeros((ROWS, LANES), F32)
    for f in range(6):
        tab_ref[pl.ds(f, ROWS, stride=8), :] = feats[11 + f]

    def wide(ref, t, n):
        return jnp.concatenate([ref[pl.ds((t * 4 + i) * n, n), :] for i in range(4)], axis=1)

    scan_low = scan % LANES
    scan_bits = [scan & LANES, scan & (2 * LANES)]
    for t in range(TM):
        parts = [tab_ref[pl.ds((4 * t + i) * 8, 8), :] for i in range(4)]
        for r in range(4 * t, 4 * t + 4):
            low_index = jnp.broadcast_to(scan_low[r : r + 1, :], (8, LANES))
            got = [jnp.take_along_axis(p, low_index, axis=1, mode="promise_in_bounds") for p in parts]
            b0, b1 = [jnp.broadcast_to(b[r : r + 1, :], (8, LANES)) != 0 for b in scan_bits]
            gat_ref[pl.ds(r * 8, 8), :] = jnp.where(b1, jnp.where(b0, got[3], got[2]), jnp.where(b0, got[1], got[0]))
    pose = [gat_ref[pl.ds(f, ROWS, stride=8), :] for f in range(6)]
    inverse = [1.0 / (1.0 + u * u) for u in pose[:3]]
    sx, sy, sz = [2.0 * u * v for u, v in zip(pose[:3], inverse)]
    cx, cy, cz = [(1.0 - u * u) * v for u, v in zip(pose[:3], inverse)]
    tr = pose[3:]
    rot = [
        [cz * cy, cz * sy * sx - sz * cx, cz * sy * cx + sz * sx],
        [sz * cy, sz * sy * sx + cz * cx, sz * sy * cx - cz * sx],
        [-sy, cy * sx, cy * cx],
    ]
    second = [[pxx, pxy, pxz], [pxy, pyy, pyz], [pxz, pyz, pzz]]
    rp = [sum(rot[i][j] * p1[j] for j in range(3)) for i in range(3)]
    half = [[sum(rot[i][k] * second[k][j] for k in range(3)) for j in range(3)] for i in range(3)]
    m1 = [rp[i] + PTS * tr[i] for i in range(3)]
    m2 = {}
    for i, j in [(0, 0), (1, 1), (2, 2), (0, 1), (0, 2), (1, 2)]:
        m2[i, j] = sum(half[i][k] * rot[j][k] for k in range(3)) + rp[i] * tr[j] + tr[i] * m1[j]
        m2[j, i] = m2[i, j]
    world = m1 + [m2[0, 0], m2[1, 1], m2[2, 2], m2[0, 1], m2[0, 2], m2[1, 2], jnp.ones((ROWS, LANES), F32)]
    for f in range(10):
        tab_ref[pl.ds(f, ROWS, stride=16), :] = world[f]

    nt = (((1,), (1,)), ((), ()))
    vox_iota = lax.broadcasted_iota(jnp.int32, (LANES, LANES), 0).astype(F32).astype(BF16)
    vox16 = jnp.where(vox < 0, -1, vox % LANES).astype(F32).astype(BF16)
    vhigh = [one_hot(vox < LANES), one_hot(vox >= LANES)]
    hots, lefts = [], []
    for t in range(TM):
        hots += [hot16(vox_iota, vox16[r : r + 1, :]) for r in range(4 * t, 4 * t + 4)]
        w = split3(wide(tab_ref, t, 16))
        masks = [jnp.concatenate([h[r : r + 1, :] for r in range(4 * t, 4 * t + 4)], axis=1) for h in vhigh]
        lefts.append(jnp.concatenate([w * m for m in masks], axis=0))
    sums = lax.dot_general(jnp.concatenate(lefts, axis=1), jnp.concatenate(hots, axis=1), nt, preferred_element_type=F32)
    sums = jnp.concatenate([sums[:48], sums[48:]], axis=1)
    sums = fold3(sums)
    count = jnp.maximum(sums[9:10] * PTS, 1.0)
    angles = angles_ref[...]
    cos, sin = jnp.cos(angles), jnp.sin(angles)
    n = [sin[0:1] * cos[1:2], sin[0:1] * sin[1:2], cos[0:1]]
    offset = (n[0] * sums[0:1] + n[1] * sums[1:2] + n[2] * sums[2:3]) / count
    quadric = (
        n[0] * n[0] * sums[3:4]
        + n[1] * n[1] * sums[4:5]
        + n[2] * n[2] * sums[5:6]
        + 2.0 * (n[0] * n[1] * sums[6:7] + n[0] * n[2] * sums[7:8] + n[1] * n[2] * sums[8:9])
    )
    cost_ref[...] = quadric / count - offset * offset
    plane = jnp.concatenate(n + [offset] + n + [offset], axis=0)
    parts = [plane[:, k * LANES : (k + 1) * LANES] for k in range(VOX // LANES)]
    sub = lax.broadcasted_iota(jnp.int32, (8, LANES), 0)
    for r in range(0, ROWS, 2):
        index = jnp.where(sub < 4, vox[r : r + 1, :], vox[r + 1 : r + 2, :])
        got = look_up(parts, jnp.maximum(index, 0))
        gat_ref[pl.ds(r * 4, 8), :] = jnp.where(index >= 0, got, 0.0)
    n0, n1, n2, d = [gat_ref[pl.ds(f, ROWS, stride=4), :] for f in range(4)]
    nb = [n0, n1, n2]

    def cross(v):
        return [v[1] * n2 - v[2] * n1, v[2] * n0 - v[0] * n2, v[0] * n1 - v[1] * n0]

    am2 = list(zip(*[cross([m2[0, j], m2[1, j], m2[2, j]]) for j in range(3)]))
    ama = [cross(am2[i]) for i in range(3)]
    am1 = cross(m1)
    terms = {}
    for i in range(3):
        for j in range(i, 3):
            terms[i, j] = ama[i][j]
            terms[3 + i, 3 + j] = PTS * nb[i] * nb[j]
        for j in range(3):
            terms[i, 3 + j] = am1[i] * nb[j]
    resid = sum(nb[i] * m1[i] for i in range(3)) - PTS * d
    grad = [sum(am2[i][j] * nb[j] for j in range(3)) - d * am1[i] for i in range(3)] + [nb[i] * resid for i in range(3)]
    features = [terms[i, j] for i in range(6) for j in range(i, 6)] + grad
    for row in range(32):
        f = row % 8 * 4 + row // 8
        if f < 28:
            feat_ref[pl.ds(row, ROWS, stride=32), :] = features[f] if f < 27 else zeros

    high = [one_hot(scan >= 256) if k else one_hot(scan < 256) for k in range(2)]
    low = (scan % 256).astype(F32).T.astype(BF16)
    scan_iota = lax.broadcasted_iota(jnp.int32, (LANES, 256), 1).astype(F32).astype(BF16)
    for t in range(TM):
        ft = wide(feat_ref, t, 32)
        hi = ft.astype(BF16)
        lo = (ft - hi.astype(F32)).astype(BF16)
        both = jnp.concatenate([hi, lo], axis=0)
        masks = [jnp.concatenate([h[r : r + 1, :] for r in range(4 * t, 4 * t + 4)], axis=1) for h in high]
        left = jnp.concatenate([both * m for m in masks], axis=0)
        hot = jnp.concatenate([hot16(scan_iota, low[:, r : r + 1]) for r in range(4 * t, 4 * t + 4)], axis=0)
        got = jnp.dot(left, hot, preferred_element_type=F32)
        for c in range(4):
            top = 64 * (c // 2)
            lanes = slice(c % 2 * LANES, (c % 2 + 1) * LANES)
            sums_c = got[top : top + 32, lanes] + got[top + 32 : top + 64, lanes]
            part = [sums_c[8 * j : 8 * j + 8] for j in range(4)]
            for g, v in enumerate(swap_groups(part)):
                out_ref[pl.ds((t * 16 + 4 * c + g) * BACK_ROWS, BACK_ROWS), :] = v[:BACK_ROWS]


def scans_kernel(scale, recv_ref, hess_ref, grad_ref):
    eight = 8 * BACK_ROWS
    acc = recv_ref[0:eight, :]
    for q in range(1, recv_ref.shape[0] // eight):
        acc = acc + recv_ref[q * eight : (q + 1) * eight, :]
    total = sum(acc[q * BACK_ROWS : (q + 1) * BACK_ROWS] for q in range(8)) * scale
    part = [total[:, j * SLOTS : (j + 1) * SLOTS] for j in range(4)]
    rows = [part[f % 4][f // 4 : f // 4 + 1] for f in range(27)]
    place = {ij: f for f, ij in enumerate([(i, j) for i in range(6) for j in range(i, 6)])}
    hess = [rows[place[min(i, j), max(i, j)]] for i in range(6) for j in range(6)]
    hess_ref[...] = jnp.concatenate(hess, axis=0).T
    grad_ref[...] = jnp.concatenate(rows[21:], axis=0)


def moments(points, voxel_ids, scan_ids, poses, devices):
    anywhere = pl.BlockSpec(memory_space=pl.ANY)
    chunks = 4
    return pl.pallas_call(
        moments_kernel,
        in_specs=[anywhere] * 4,
        out_shape=pltpu.VMEM((devices * SENT_ROWS, LANES), F32),
        out_specs=pl.BlockSpec(memory_space=pltpu.VMEM),
        scratch_shapes=[
            pltpu.VMEM((9, ROWS, LANES), F32),
            pltpu.VMEM(points.shape, F32),
            pltpu.VMEM((ROWS, LANES), jnp.int32),
            pltpu.VMEM((ROWS, LANES), jnp.int32),
            pltpu.VMEM(poses.shape, F32),
            pltpu.SemaphoreType.DMA((chunks,)),
            pltpu.SemaphoreType.DMA((3,)),
        ],
        compiler_params=pltpu.CompilerParams(vmem_limit_bytes=56 * 1024 * 1024),
    )(points, voxel_ids.reshape(ROWS, LANES), scan_ids.reshape(ROWS, LANES), poses)


def owner(recv, normal_angles, devices):
    return pl.pallas_call(
        owner_kernel,
        out_shape=(
            jax.ShapeDtypeStruct((devices * BACK_ROWS, LANES), F32),
            jax.ShapeDtypeStruct((1, VOX), F32),
        ),
        scratch_shapes=[
            pltpu.VMEM((ROWS * 16, LANES), F32),
            pltpu.VMEM((ROWS * 16, LANES), F32),
            pltpu.VMEM((ROWS * 32, LANES), F32),
        ],
        compiler_params=pltpu.CompilerParams(vmem_limit_bytes=32 * 1024 * 1024),
    )(recv, normal_angles)


def local(points, poses, normal_angles, voxel_ids, scan_ids):
    axes = ("tm", "map")
    blocks = points.shape[1]
    devices = lax.axis_size(axes)
    sent = moments(points, voxel_ids, scan_ids, poses, devices)
    recv = lax.all_to_all(sent.reshape(devices, 1, SENT_ROWS * LANES), axes, 0, 0, tiled=True)
    recv = recv.reshape(devices * SENT_ROWS, LANES)
    shares, cost = owner(recv, normal_angles, devices)
    arrived = lax.all_to_all(shares.reshape(devices, 1, BACK_ROWS * LANES), axes, 0, 0, tiled=True)
    arrived = arrived.reshape(devices * BACK_ROWS, LANES)
    all_scans = poses.shape[1] * devices
    scale = all_scans / (blocks * devices * PTS)
    hess, grad = pl.pallas_call(
        functools.partial(scans_kernel, scale),
        out_shape=(
            jax.ShapeDtypeStruct((SLOTS, 36), F32),
            jax.ShapeDtypeStruct((6, SLOTS), F32),
        ),
        compiler_params=pltpu.CompilerParams(vmem_limit_bytes=8 * 1024 * 1024),
    )(arrived)
    return hess.T, grad, cost.reshape(VOX)


def solution(mesh):
    return jax.shard_map(
        local,
        mesh=mesh,
        in_specs=(
            P(None, ("tm", "map"), None),
            P(None, ("tm", "map")),
            P(None, ("tm", "map")),
            P(("tm", "map")),
            P(("tm", "map")),
        ),
        out_specs=(P(None, ("tm", "map")), P(None, ("tm", "map")), P(("tm", "map"))),
        check_vma=False,
    )
```
